512 devices in a mesh: row: 32 (over z_lo, x, core), col: 16 (over z_hi, y).
Axes of the slice: x: 4, y: 8, z: 8 (z_hi: 2, z_lo: 4; z = z_hi * 4 + z_lo), core: 2. Of those that a mesh axis runs over, the one named last changes fastest.
Arguments:
- features: bfloat16 [65536, 512], P(('row', 'col')), may hold values from -6 to 6
- weight: bfloat16 [512, 512], replicated, may hold values from -0.25 to 0.25
- bias_term: float32 [512], replicated, may hold values from -3 to 3
- cotangent: bfloat16 [65536, 512], P(('row', 'col')), may hold values from -0.125 to 0.125
- tile_values: bfloat16 [32, 16, 11, 256, 256], P('row', 'col'), may hold values from -0.078125 to 0.078125
- tile_rows: int32 [32, 16, 11], P('row', 'col'), may hold values from 0 to 7
- tile_cols: int32 [32, 16, 11], P('row', 'col'), may hold values from 0 to 15
- tile_count: int32 [32, 16], P('row', 'col'), may hold values from 1 to 11, as said below
Outputs:
- activations: bfloat16 [65536, 512], P(('row', 'col'))
- weight_grad: float32 [512, 512], replicated
- bias_grad: float32 [512], replicated
The draws below stay inside these ranges and needn't reach their ends.
Inputs may be any that keep to these rules, and one draw needn't show every extreme that they name: Slots from tile_count on hold no tile; some grid cell uses all 11 slots in every draw.
All inputs are finite; a program needn't handle non-finite values.
Results may differ from the reference program's by a relative error of at most 0.017.
Values may be sent and summed in bfloat16 or wider, within the bound.
No kernel may reach another device: no remote copies, remote signals or barrier semaphores. Data moves between devices by JAX's collectives and lax.ppermute only.
A program may use at most 64 MiB of HBM per device.

```python
import jax
import jax.numpy as jnp
from jax import lax

WIDTH = 512
TILE = 256
NODES_DEV = 128
TILES = 11
GRID_ROWS = 32
GRID_COLS = 16
NODES = 65536
TILE_ROWS = 8
TILE_COLS = 16


def draw_tile_count(key, part):
    key = jax.random.fold_in(key, 7)
    first_key, second_key = jax.random.split(key)
    samples = jax.random.randint(first_key, (3, GRID_ROWS * GRID_COLS), 1, TILES + 1)
    lowest = jnp.min(samples, axis=0)
    chosen = jax.random.randint(second_key, (), 0, GRID_ROWS * GRID_COLS)
    filled = jnp.where(jnp.arange(GRID_ROWS * GRID_COLS) == chosen, TILES, lowest)
    return filled.reshape(GRID_ROWS, GRID_COLS).astype(jnp.int32)


def place_ends(array, rng, smallest, top_value):
    spot = [jax.random.randint(jax.random.fold_in(rng, axis), (), 0, length) for axis, length in enumerate(array.shape)]
    main_axis = array.shape.index(max(array.shape))
    beside = spot[:main_axis] + [(spot[main_axis] + 1) % array.shape[main_axis]] + spot[main_axis + 1:]
    return array.at[tuple(spot)].set(smallest).at[tuple(beside)].set(top_value)


def steps_of(own_key, extent, cuts, least, largest):
    gain, own = 1.0, jax.random.fold_in(own_key, 6)
    for position, blocks in cuts:
        steps = jnp.exp(jax.random.uniform(jax.random.fold_in(own, position), (blocks,), jnp.float32, least / len(cuts), largest / len(cuts)))
        gain = gain * jnp.repeat(steps, extent[position] // blocks).reshape([-1 if axis == position else 1 for axis in range(len(extent))])
    return gain


def scatter_about(stream_key, dims, width, bound, cuts=(), kind=jnp.bfloat16):
    values = width * jax.random.normal(stream_key, dims, jnp.float32)
    if cuts:
        values = values * steps_of(stream_key, dims, cuts, -0.22, 0.18)
    return jnp.clip(values, -bound, bound).astype(kind)


def setup_inputs(seed: int = 0) -> dict:
    splits = jax.random.split(jax.random.key(seed), 9)
    features = scatter_about(splits[0], (NODES, WIDTH), 1.0, 6.0, ((0, 512),))
    weight = scatter_about(splits[1], (WIDTH, WIDTH), WIDTH ** -0.5, 0.25)
    bias_term = scatter_about(splits[2], (WIDTH,), 0.5, 3.0, (), jnp.float32)
    cotangent = scatter_about(splits[3], (NODES, WIDTH), (2.0 * NODES ** -0.5), 0.125, ((0, 512),))
    tile_values = scatter_about(splits[4], (GRID_ROWS, GRID_COLS, TILES, TILE, TILE), (TILES * TILE * TILE // NODES_DEV) ** -0.5, 0.078125, ((0, 32), (1, 16)))
    tile_rows = place_ends(jax.random.randint(splits[5], (GRID_ROWS, GRID_COLS, TILES), 0, TILE_ROWS), jax.random.fold_in(splits[5], 1), 0, TILE_ROWS - 1).astype(jnp.int32)
    tile_cols = place_ends(jax.random.randint(splits[6], (GRID_ROWS, GRID_COLS, TILES), 0, TILE_COLS), jax.random.fold_in(splits[6], 1), 0, TILE_COLS - 1).astype(jnp.int32)
    tile_count = draw_tile_count(jax.random.fold_in(splits[8], 71), 0)
    return dict(features=features, weight=weight, bias_term=bias_term, cotangent=cotangent, tile_values=tile_values, tile_rows=tile_rows, tile_cols=tile_cols, tile_count=tile_count)


def cell_partial(tile_mats, row_ids, col_ids, used, column_block):
    stacked = column_block.reshape(TILE_COLS, TILE, WIDTH)
    windows = jnp.take(stacked, col_ids, axis=0).astype(jnp.float32)
    products = jnp.einsum("kab,kbf->kaf", tile_mats.astype(jnp.float32), windows, precision=lax.Precision.HIGHEST)
    live_slots = jnp.arange(TILES) < used
    selector = jnp.logical_and(row_ids[None, :] == jnp.arange(TILE_ROWS)[:, None], live_slots[None, :]).astype(jnp.float32)
    summed = jnp.einsum("rk,kaf->raf", selector, products, precision=lax.Precision.HIGHEST)
    return summed.reshape(TILE_ROWS * TILE, WIDTH)


def reference(features, weight, bias_term, cotangent, tile_values, tile_rows, tile_cols, tile_count):
    grid_view = features.reshape(GRID_ROWS, GRID_COLS, NODES_DEV, WIDTH)

    def one_row(row_index):
        def add_cell(running, col_index):
            column_block = grid_view[:, col_index].reshape(GRID_ROWS * NODES_DEV, WIDTH)
            term = cell_partial(tile_values[row_index, col_index], tile_rows[row_index, col_index],
                                tile_cols[row_index, col_index], tile_count[row_index, col_index], column_block)
            term_rounded = lax.optimization_barrier(term.astype(jnp.bfloat16))
            return running + term_rounded.astype(jnp.float32), None

        start_sum = jnp.zeros((TILE_ROWS * TILE, WIDTH), jnp.float32)
        return lax.scan(add_cell, start_sum, jnp.arange(GRID_COLS))[0]

    aggregated = lax.map(one_row, jnp.arange(GRID_ROWS)).reshape(NODES, WIDTH)
    rounded = aggregated.astype(jnp.bfloat16)
    preact = jnp.dot(rounded, weight, preferred_element_type=jnp.float32) + bias_term
    activations = jax.nn.silu(preact).astype(jnp.bfloat16)
    sigmoid_part = jax.nn.sigmoid(preact)
    grad_preact = cotangent.astype(jnp.float32) * sigmoid_part * (1.0 + preact * (1.0 - sigmoid_part))
    grad_rounded = grad_preact.astype(jnp.bfloat16)
    weight_grad = jnp.dot(rounded.T, grad_rounded, preferred_element_type=jnp.float32)
    bias_grad = jnp.sum(grad_preact, axis=0)
    return activations, weight_grad, bias_grad
```

```python
import jax
import jax.numpy as jnp
from jax import lax
from jax.experimental import pallas as pl
from jax.experimental.pallas import tpu as pltpu
from jax.sharding import PartitionSpec as P

F32 = jnp.float32
BF16 = jnp.bfloat16
LANES = 128
VMEM = pl.BlockSpec(memory_space=pltpu.VMEM)
SMEM = pl.BlockSpec(memory_space=pltpu.SMEM)
PARAMS = pltpu.CompilerParams(vmem_limit_bytes=40 * 1024 * 1024)


def tile_kernel(rows_ref, cols_ref, count_ref, tiles_ref, block_ref, out_ref, total):
    size = tiles_ref.shape[1]
    total[...] = jnp.zeros_like(total)

    def step(slot, carry):
        rows = pl.ds(pl.multiple_of(rows_ref[slot] * size, size), size)
        window = pl.ds(pl.multiple_of(cols_ref[slot] * size, size), size)
        total[rows, :] += jnp.dot(
            tiles_ref[slot], block_ref[window, :], preferred_element_type=F32
        )
        return carry

    lax.fori_loop(0, count_ref[0], step, 0)
    out_ref[...] = total[...].astype(BF16)


def split_column(column):
    high = column.astype(BF16)
    low = (column - high.astype(F32)).astype(BF16)
    lane = lax.broadcasted_iota(jnp.int32, column.shape, 1)
    return jnp.where(lane == 0, high.astype(F32), jnp.where(lane == 1, low.astype(F32), 0.0)).astype(BF16)


def node_kernel(shares_ref, weight_ref, bias_ref, cot_ref, act_ref, grads_ref):
    width = weight_ref.shape[1]
    total = shares_ref[0].astype(F32)
    for share in range(1, shares_ref.shape[0]):
        total = total + shares_ref[share].astype(F32)
    aggregated = total.astype(BF16)
    preact = jnp.dot(aggregated, weight_ref[...], preferred_element_type=F32) + bias_ref[...]
    sigmoid_part = jax.nn.sigmoid(preact)
    act_ref[...] = (preact * sigmoid_part).astype(BF16)
    grad = cot_ref[...].astype(F32) * sigmoid_part * (1.0 + preact * (1.0 - sigmoid_part))
    rounded = grad.astype(BF16)
    rest = (grad - rounded.astype(F32)).astype(BF16)
    over_nodes = (((0,), (0,)), ((), ()))
    grads_ref[:, :width] = lax.dot_general(
        aggregated, rounded, over_nodes, preferred_element_type=F32
    ).astype(BF16)
    ones = jnp.ones((grad.shape[0], LANES), BF16)
    column = lax.dot_general(rounded, ones, over_nodes, preferred_element_type=F32)
    column = column + lax.dot_general(rest, ones, over_nodes, preferred_element_type=F32)
    grads_ref[:, width:] = split_column(column)


def sum_kernel(parts_ref, out_ref):
    width = parts_ref.shape[2] - LANES
    total = parts_ref[0].astype(F32)
    for part in range(1, parts_ref.shape[0]):
        total = total + parts_ref[part].astype(F32)
    main = total[:, :width].astype(BF16)
    column = total[:, width : width + 1] + total[:, width + 1 : width + 2]
    side = split_column(jnp.broadcast_to(column, (column.shape[0], LANES)))
    for copy in range(out_ref.shape[0]):
        out_ref[copy, :, :width] = main
        out_ref[copy, :, width:] = side


def sum_parts(parts, copies):
    return pl.pallas_call(
        sum_kernel,
        out_shape=jax.ShapeDtypeStruct((copies,) + parts.shape[1:], BF16),
        in_specs=[VMEM],
        out_specs=VMEM,
        compiler_params=PARAMS,
    )(parts)


def per_device(
    features, weight, bias_term, cotangent, tile_values, tile_rows, tile_cols, tile_count
):
    n_rows, n_cols = lax.axis_size("row"), lax.axis_size("col")
    nodes, width = features.shape
    height = n_cols * nodes
    gathered = lax.all_gather(features, "row", axis=0, tiled=True)
    term = pl.pallas_call(
        tile_kernel,
        out_shape=jax.ShapeDtypeStruct((height, width), BF16),
        in_specs=[SMEM, SMEM, SMEM, VMEM, VMEM],
        out_specs=VMEM,
        scratch_shapes=[pltpu.VMEM((height, width), F32)],
        compiler_params=PARAMS,
    )(tile_rows[0, 0], tile_cols[0, 0], tile_count[0], tile_values[0, 0], gathered)
    shares = lax.all_to_all(term.reshape(n_cols, nodes, width), "col", 0, 0)
    activations, grads = pl.pallas_call(
        node_kernel,
        out_shape=(
            jax.ShapeDtypeStruct((nodes, width), BF16),
            jax.ShapeDtypeStruct((width, width + LANES), BF16),
        ),
        in_specs=[VMEM] * 4,
        out_specs=(VMEM, VMEM),
        compiler_params=PARAMS,
    )(shares, weight, bias_term[None, :], cotangent)
    chunk = width // n_rows
    grads = lax.all_to_all(grads.reshape(n_rows, chunk, width + LANES), "row", 0, 0)
    grads = lax.all_to_all(sum_parts(grads, n_cols), "col", 0, 0)
    grads = lax.all_to_all(sum_parts(grads, n_rows), "row", 0, 0)
    grads = grads.reshape(width, width + LANES).astype(F32)
    weight_grad = grads[:, :width]
    bias_grad = grads[:, width] + grads[:, width + 1]
    return activations, weight_grad, bias_grad


def solution(mesh):
    return jax.shard_map(
        per_device,
        mesh=mesh,
        in_specs=(
            P(("row", "col"), None),
            P(),
            P(),
            P(("row", "col"), None),
            P("row", "col", None, None, None),
            P("row", "col", None),
            P("row", "col", None),
            P("row", "col"),
        ),
        out_specs=(P(("row", "col"), None), P(), P()),
        check_vma=False,
    )
```

```python
import jax
import jax.numpy as jnp
from jax import lax
from jax.experimental import pallas as pl
from jax.experimental.pallas import tpu as pltpu
from jax.sharding import Mesh, PartitionSpec as P

F32 = jnp.float32
BF16 = jnp.bfloat16
LANES = 128
VMEM = pl.BlockSpec(memory_space=pltpu.VMEM)
SMEM = pl.BlockSpec(memory_space=pltpu.SMEM)
ANY = pl.BlockSpec(memory_space=pl.ANY)
PARAMS = pltpu.CompilerParams(vmem_limit_bytes=40 * 1024 * 1024)
AXES = ("z_lo", "x", "core", "z_hi", "y_pair", "y_odd")
ROW = ("z_lo", "x", "core")
COL = ("z_hi", "y_pair", "y_odd")
Y = ("y_pair", "y_odd")
Z_LO, X, Y_SIZE = 4, 4, 8


def tile_kernel(
    place_ref, rows_ref, cols_ref, count_ref, tiles_ref, *refs
):
    own, other = refs[:5], refs[5:10]
    keep_ref, left_ref, right_ref, tiles, windows, total, sems = refs[10:]
    slots, size, _ = tiles.shape
    half = size // 2
    lanes = left_ref.shape[2]
    z, x, core, odd = place_ref[0], place_ref[1], place_ref[2], place_ref[3]
    used = count_ref[0]

    def tile_copy(slot):
        return pltpu.make_async_copy(tiles_ref.at[slot], tiles.at[slot], sems.at[0, slot])

    def half_copy(ref, index, slot, which):
        return pltpu.make_async_copy(ref.at[index], windows.at[slot, which], sems.at[1 + which, slot])

    def fetch(slot, carry):
        tile_copy(slot).start()
        chip = cols_ref[slot]
        dz = lax.rem(z - chip // X + Z_LO, Z_LO)
        dx = lax.rem(x - lax.rem(chip, X) + X, X)
        late = dz >= Z_LO // 2
        cases = (
            (dx == 0, 0, dz),
            (dx == 1, 1, dz),
            (dx == 3, 2, dz),
            (jnp.logical_and(dx == 2, jnp.logical_not(late)), 3, dz),
            (jnp.logical_and(dx == 2, late), 4, dz - Z_LO // 2),
        )
        for condition, block, index in cases:

            @pl.when(condition)
            def _():
                half_copy(own[block], index, slot, core).start()
                half_copy(other[block], index, slot, 1 - core).start()

        return carry

    lax.fori_loop(0, used, fetch, 0)
    total[...] = jnp.zeros_like(total)

    def step(slot, carry):
        tile_copy(slot).wait()
        half_copy(own[0], 0, slot, 0).wait()
        half_copy(own[0], 0, slot, 1).wait()
        window = windows[slot].reshape(size, windows.shape[3])
        total[rows_ref[slot]] += jnp.dot(tiles[slot], window, preferred_element_type=F32)
        return carry

    lax.fori_loop(0, used, step, 0)
    mine = pl.multiple_of(odd * half, half)
    theirs = pl.multiple_of((1 - odd) * half, half)
    for row in range(total.shape[0]):
        keep_ref[row] = total[row, pl.ds(mine, half), :].astype(BF16)
        send = total[row, pl.ds(theirs, half), :].astype(BF16)
        left_ref[row] = send[:, :lanes]
        right_ref[row] = send[:, lanes:]


def pair_kernel(keep_ref, left_ref, right_ref, out_ref):
    lanes = left_ref.shape[2]
    keep = keep_ref[...].astype(F32)
    out_ref[:, :, :lanes] = (keep[:, :, :lanes] + left_ref[...].astype(F32)).astype(BF16)
    out_ref[:, :, lanes:] = (keep[:, :, lanes:] + right_ref[...].astype(F32)).astype(BF16)


def split_column(column):
    high = column.astype(BF16)
    low = (column - high.astype(F32)).astype(BF16)
    lane = lax.broadcasted_iota(jnp.int32, column.shape, 1)
    return jnp.where(lane == 0, high.astype(F32), jnp.where(lane == 1, low.astype(F32), 0.0)).astype(BF16)


def node_kernel(shares_ref, weight_ref, bias_ref, cot_ref, act_ref, grads_ref):
    width = weight_ref.shape[1]
    total = shares_ref[0].astype(F32)
    for share in range(1, shares_ref.shape[0]):
        total = total + shares_ref[share].astype(F32)
    aggregated = total.astype(BF16)
    preact = jnp.dot(aggregated, weight_ref[...], preferred_element_type=F32) + bias_ref[...]
    sigmoid_part = jax.nn.sigmoid(preact)
    act_ref[...] = (preact * sigmoid_part).astype(BF16)
    grad = cot_ref[...].astype(F32) * sigmoid_part * (1.0 + preact * (1.0 - sigmoid_part))
    rounded = grad.astype(BF16)
    rest = (grad - rounded.astype(F32)).astype(BF16)
    over_nodes = (((0,), (0,)), ((), ()))
    grads_ref[:, :width] = lax.dot_general(
        aggregated, rounded, over_nodes, preferred_element_type=F32
    ).astype(BF16)
    ones = jnp.ones((grad.shape[0], LANES), BF16)
    column = lax.dot_general(rounded, ones, over_nodes, preferred_element_type=F32)
    column = column + lax.dot_general(rest, ones, over_nodes, preferred_element_type=F32)
    grads_ref[:, width:] = split_column(column)


def sum_kernel(parts_ref, out_ref):
    width = parts_ref.shape[2] - LANES
    total = parts_ref[0].astype(F32)
    for part in range(1, parts_ref.shape[0]):
        total = total + parts_ref[part].astype(F32)
    main = total[:, :width].astype(BF16)
    column = total[:, width : width + 1] + total[:, width + 1 : width + 2]
    side = split_column(jnp.broadcast_to(column, (column.shape[0], LANES)))
    for copy in range(out_ref.shape[0]):
        out_ref[copy, :, :width] = main
        out_ref[copy, :, width:] = side


def sum_parts(parts, copies):
    return pl.pallas_call(
        sum_kernel,
        out_shape=jax.ShapeDtypeStruct((copies,) + parts.shape[1:], BF16),
        in_specs=[VMEM],
        out_specs=VMEM,
        compiler_params=PARAMS,
    )(parts)


def shift(array, axis, size, by):
    return lax.ppermute(array, axis, [(i, (i + by) % size) for i in range(size)])


def gather_row(features):
    near = [features] + [shift(features, "z_lo", Z_LO, by) for by in range(1, Z_LO)]
    own = jnp.stack(near)
    left, right = shift(own, "x", X, 1), shift(own, "x", X, -1)
    far_left = shift(left[: Z_LO // 2], "x", X, 1)
    far_right = shift(right[Z_LO // 2 :], "x", X, -1)
    blocks = [own, left, right, far_left, far_right]
    return blocks, [shift(block, "core", 2, 1) for block in blocks]


def per_device(
    features, weight, bias_term, cotangent, tile_values, tile_rows, tile_cols, tile_count
):
    n_rows, n_cols = lax.axis_size(ROW), lax.axis_size(COL)
    nodes, width = features.shape
    _, _, slots, size, _ = tile_values.shape
    n_tiles = n_cols * nodes // size
    own, other = gather_row(features)
    place = jnp.stack([lax.axis_index(axis) for axis in ("z_lo", "x", "core", "y_odd")])
    keep, left, right = pl.pallas_call(
        tile_kernel,
        out_shape=(
            jax.ShapeDtypeStruct((n_tiles, nodes, width), BF16),
            jax.ShapeDtypeStruct((n_tiles, nodes, width // 2), BF16),
            jax.ShapeDtypeStruct((n_tiles, nodes, width // 2), BF16),
        ),
        in_specs=[SMEM] * 4 + [ANY] * 11,
        out_specs=(VMEM, VMEM, VMEM),
        scratch_shapes=[
            pltpu.VMEM((slots, size, size), BF16),
            pltpu.VMEM((slots, 2, size // 2, width), BF16),
            pltpu.VMEM((n_tiles, size, width), F32),
            pltpu.SemaphoreType.DMA((3, slots)),
        ],
        compiler_params=PARAMS,
    )(
        place.astype(jnp.int32),
        tile_rows[0, 0],
        tile_cols[0, 0],
        tile_count[0],
        tile_values[0, 0],
        *own,
        *other,
    )
    left = lax.ppermute(left, Y, [(i, i ^ 1) for i in range(Y_SIZE)])
    right = lax.ppermute(right, Y, [(i, (i + 2 * (i % 2) - 1) % Y_SIZE) for i in range(Y_SIZE)])
    paired = pl.pallas_call(
        pair_kernel,
        out_shape=jax.ShapeDtypeStruct((n_tiles, nodes, width), BF16),
        in_specs=[VMEM] * 3,
        out_specs=VMEM,
        compiler_params=PARAMS,
    )(keep, left, right)
    shares = lax.all_to_all(paired, ("z_hi", "y_pair"), 0, 0)
    activations, grads = pl.pallas_call(
        node_kernel,
        out_shape=(
            jax.ShapeDtypeStruct((nodes, width), BF16),
            jax.ShapeDtypeStruct((width, width + LANES), BF16),
        ),
        in_specs=[VMEM] * 4,
        out_specs=(VMEM, VMEM),
        compiler_params=PARAMS,
    )(shares, weight, bias_term[None, :], cotangent)
    chunk = width // n_rows
    grads = lax.all_to_all(grads.reshape(n_rows, chunk, width + LANES), ROW, 0, 0)
    grads = lax.all_to_all(sum_parts(grads, n_cols), COL, 0, 0)
    grads = lax.all_to_all(sum_parts(grads, n_rows), ROW, 0, 0)
    grads = grads.reshape(width, width + LANES).astype(F32)
    weight_grad = grads[:, :width]
    bias_grad = grads[:, width] + grads[:, width + 1]
    return activations, weight_grad, bias_grad


def solution(mesh):
    cut = Mesh(mesh.devices.reshape(Z_LO, X, 2, 2, Y_SIZE // 2, 2), AXES)
    everywhere = P(AXES, None)
    return jax.shard_map(
        per_device,
        mesh=cut,
        in_specs=(
            everywhere,
            P(),
            P(),
            everywhere,
            P(ROW, COL, None, None, None),
            P(ROW, COL, None),
            P(ROW, COL, None),
            P(ROW, COL),
        ),
        out_specs=(everywhere, P(), P()),
        check_vma=False,
    )
```

```python
import jax
import jax.numpy as jnp
from jax import lax
from jax.experimental import pallas as pl
from jax.experimental.pallas import tpu as pltpu
from jax.sharding import Mesh, PartitionSpec as P

F32 = jnp.float32
BF16 = jnp.bfloat16
LANES = 128
VMEM = pl.BlockSpec(memory_space=pltpu.VMEM)
SMEM = pl.BlockSpec(memory_space=pltpu.SMEM)
ANY = pl.BlockSpec(memory_space=pl.ANY)
PARAMS = pltpu.CompilerParams(vmem_limit_bytes=40 * 1024 * 1024)
AXES = ("z_lo", "x", "core", "z_hi", "y_pair", "y_odd")
ROW = ("z_lo", "x", "core")
COL = ("z_hi", "y_pair", "y_odd")
QUAD = ("core", "y_odd")
REST = ("z_hi", "y_pair")
PLANE = ("x", "core", "y_pair", "y_odd")
DEPTH = ("z_lo", "z_hi")
SIZES = (4, 4, 2, 2, 4, 2)
SIDE = 16


def quarter_kernel(features_ref, side_ref, out_ref):
    nodes = features_ref.shape[0]
    for part in range(out_ref.shape[0]):
        out_ref[part, :nodes, :] = features_ref[:, part * LANES : (part + 1) * LANES]
        out_ref[part, nodes:, :] = side_ref[...]


def tile_kernel(place_ref, meta_ref, *refs):
    given, block_ref, out_ref, tiles, total, sems = refs[:4], refs[4], refs[5], refs[6], refs[7], refs[8]
    _, slots, size, _ = tiles.shape
    n_x = block_ref.shape[0]
    core, odd = place_ref[0], place_ref[1]

    def tile_copy(which, slot):
        return pltpu.make_async_copy(
            given[which].at[slot], tiles.at[which, slot], sems.at[which, slot]
        )

    def cell_of(which):
        cell_core, cell_odd = (core + which // 2) % 2, (odd + which % 2) % 2
        return cell_core, cell_odd, cell_core * 2 + cell_odd

    for which in range(4):

        def fetch(slot, carry):
            tile_copy(which, slot).start()
            return carry

        lax.fori_loop(0, meta_ref[cell_of(which)[2], 2, 0], fetch, 0)
    total[...] = jnp.zeros_like(total)
    for which in range(4):
        cell_core, cell_odd, cell = cell_of(which)

        def step(slot, carry):
            tile_copy(which, slot).wait()
            chip = meta_ref[cell, 1, slot]
            z, x = chip // n_x, lax.rem(chip, n_x)
            window = jnp.concatenate(
                [block_ref[x, z, cell_odd], block_ref[x, z, 2 + cell_odd]], axis=0
            )
            total[cell_core, meta_ref[cell, 0, slot]] += jnp.dot(
                tiles[which, slot], window, preferred_element_type=F32
            )
            return carry

        lax.fori_loop(0, meta_ref[cell, 2, 0], step, 0)
    for row in range(total.shape[1]):
        for cell_core in range(2):
            out_ref[row, cell_core] = total[cell_core, row].astype(BF16)


def add_kernel(parts_ref, out_ref):
    total = parts_ref[0].astype(F32)
    for part in range(1, parts_ref.shape[0]):
        total = total + parts_ref[part].astype(F32)
    out_ref[...] = total.astype(BF16)


def split_column(column):
    high = column.astype(BF16)
    low = (column - high.astype(F32)).astype(BF16)
    lane = lax.broadcasted_iota(jnp.int32, column.shape, 1)
    return jnp.where(lane == 0, high.astype(F32), jnp.where(lane == 1, low.astype(F32), 0.0)).astype(BF16)


def node_kernel(shares_ref, weight_ref, bias_ref, cot_ref, act_ref, grads_ref):
    width = weight_ref.shape[1]
    aggregated = jnp.concatenate([shares_ref[part] for part in range(shares_ref.shape[0])], axis=1)
    preact = jnp.dot(aggregated, weight_ref[...], preferred_element_type=F32) + bias_ref[...]
    sigmoid_part = jax.nn.sigmoid(preact)
    act_ref[...] = (preact * sigmoid_part).astype(BF16)
    grad = cot_ref[...].astype(F32) * sigmoid_part * (1.0 + preact * (1.0 - sigmoid_part))
    rounded = grad.astype(BF16)
    rest = (grad - rounded.astype(F32)).astype(BF16)
    over_nodes = (((0,), (0,)), ((), ()))
    grads_ref[:, :width] = lax.dot_general(
        aggregated, rounded, over_nodes, preferred_element_type=F32
    ).astype(BF16)
    ones = jnp.ones((grad.shape[0], LANES), BF16)
    column = lax.dot_general(rounded, ones, over_nodes, preferred_element_type=F32)
    column = column + lax.dot_general(rest, ones, over_nodes, preferred_element_type=F32)
    grads_ref[:, width:] = split_column(column)


def sum_kernel(parts_ref, out_ref):
    width = parts_ref.shape[2] - LANES
    total = parts_ref[0].astype(F32)
    for part in range(1, parts_ref.shape[0]):
        total = total + parts_ref[part].astype(F32)
    main = total[:, :width].astype(BF16)
    column = total[:, width : width + 1] + total[:, width + 1 : width + 2]
    side = split_column(jnp.broadcast_to(column, (column.shape[0], LANES)))
    for copy in range(out_ref.shape[0]):
        out_ref[copy, :, :width] = main
        out_ref[copy, :, width:] = side


def sum_parts(parts, copies):
    return pl.pallas_call(
        sum_kernel,
        out_shape=jax.ShapeDtypeStruct((copies,) + parts.shape[1:], BF16),
        in_specs=[VMEM],
        out_specs=VMEM,
        compiler_params=PARAMS,
    )(parts)


def last_kernel(parts_ref, weight_ref, bias_ref):
    width = weight_ref.shape[1]
    weight_ref[...] = parts_ref[:, :width].astype(F32)
    side = jnp.transpose(parts_ref[:, width:].astype(F32))
    bias_ref[...] = side[0:1] + side[1:2]


def call(kernel, out, *args):
    shapes = jax.tree.map(lambda o: jax.ShapeDtypeStruct(*o), out, is_leaf=lambda o: isinstance(o[0], tuple) and not isinstance(o[1], tuple))
    specs = jax.tree.map(lambda o: VMEM, shapes)
    return pl.pallas_call(
        kernel, out_shape=shapes, in_specs=[VMEM] * len(args), out_specs=specs, compiler_params=PARAMS
    )(*args)


def swap(array, axis):
    return lax.ppermute(array, axis, [(0, 1), (1, 0)])


def per_device(
    features, weight, bias_term, cotangent, tile_values, tile_rows, tile_cols, tile_count
):
    nodes, width = features.shape
    _, _, slots, size, _ = tile_values.shape
    n_z, n_x = lax.axis_size("z_lo"), lax.axis_size("x")
    n_rest = lax.axis_size(REST)
    tiles = tile_values[0, 0]
    tiles_y = swap(tiles, "y_odd")
    tiles_core = swap(tiles, "core")
    tiles_both = swap(tiles_y, "core")
    ints = [tile_rows[0, 0], tile_cols[0, 0], jnp.broadcast_to(tile_count[0], (slots,))]
    side = jnp.pad(jnp.stack(ints), ((0, SIDE - 3), (0, LANES - slots))).astype(BF16)
    quarters = call(quarter_kernel, ((4, nodes + SIDE, LANES), BF16), features, side)
    quarters = lax.all_to_all(quarters, QUAD, 0, 0)
    meta = quarters[:, nodes : nodes + 3, :slots].astype(jnp.int32)
    near = lax.all_gather(quarters[:, :nodes], "z_lo", axis=0)
    blocks = lax.all_to_all(jnp.broadcast_to(near[None], (n_x,) + near.shape), "x", 0, 0)
    place = jnp.stack([lax.axis_index(axis) for axis in QUAD]).astype(jnp.int32)
    term = pl.pallas_call(
        tile_kernel,
        out_shape=jax.ShapeDtypeStruct((n_rest, 2, size, LANES), BF16),
        in_specs=[SMEM, SMEM] + [ANY] * 4 + [VMEM],
        out_specs=VMEM,
        scratch_shapes=[
            pltpu.VMEM((4, slots, size, size), BF16),
            pltpu.VMEM((2, n_rest, size, LANES), F32),
            pltpu.SemaphoreType.DMA((4, slots)),
        ],
        compiler_params=PARAMS,
    )(place, meta, tiles, tiles_y, tiles_core, tiles_both, blocks)
    shares = lax.all_to_all(term, REST, 0, 0)
    shares = call(add_kernel, ((2, size, LANES), BF16), shares)
    shares = lax.all_to_all(shares.reshape(4, nodes, LANES), QUAD, 0, 0)
    activations, grads = call(
        node_kernel,
        (((nodes, width), BF16), ((width, width + LANES), BF16)),
        shares,
        weight,
        bias_term[None, :],
        cotangent,
    )
    n_plane, n_depth = lax.axis_size(PLANE), lax.axis_size(DEPTH)
    grads = lax.all_to_all(grads.reshape(n_plane, width // n_plane, width + LANES), PLANE, 0, 0)
    grads = lax.all_to_all(sum_parts(grads, n_depth), DEPTH, 0, 0)
    grads = lax.all_to_all(sum_parts(grads, n_plane), PLANE, 0, 0)
    weight_grad, bias_grad = call(
        last_kernel,
        (((width, width), F32), ((1, width), F32)),
        grads.reshape(width, width + LANES),
    )
    return activations, weight_grad, bias_grad[0]


def solution(mesh):
    cut = Mesh(mesh.devices.reshape(SIZES), AXES)
    everywhere = P(AXES, None)
    return jax.shard_map(
        per_device,
        mesh=cut,
        in_specs=(
            everywhere,
            P(),
            P(),
            everywhere,
            P(ROW, COL, None, None, None),
            P(ROW, COL, None),
            P(ROW, COL, None),
            P(ROW, COL),
        ),
        out_specs=(everywhere, P(), P()),
        check_vma=False,
    )
```

```python
import jax
import jax.numpy as jnp
from jax import lax
from jax.experimental import pallas as pl
from jax.experimental.pallas import tpu as pltpu
from jax.sharding import Mesh, PartitionSpec as P

F32 = jnp.float32
BF16 = jnp.bfloat16
LANES = 128
VMEM = pl.BlockSpec(memory_space=pltpu.VMEM)
SMEM = pl.BlockSpec(memory_space=pltpu.SMEM)
ANY = pl.BlockSpec(memory_space=pl.ANY)
PARAMS = pltpu.CompilerParams(vmem_limit_bytes=40 * 1024 * 1024)
AXES = ("z_lo", "x", "core", "z_hi", "y_pair", "y_odd")
ROW = ("z_lo", "x", "core")
COL = ("z_hi", "y_pair", "y_odd")
QUAD = ("core", "y_odd")
REST = ("z_hi", "y_pair")
PLANE = ("x", "y_pair")
DEPTH = ("z_lo", "z_hi")
SIZES = (4, 4, 2, 2, 4, 2)
SIDE = 16


def quarter_kernel(features_ref, side_ref, out_ref):
    nodes = features_ref.shape[0]
    for part in range(out_ref.shape[0]):
        out_ref[part, :nodes, :] = features_ref[:, part * LANES : (part + 1) * LANES]
        out_ref[part, nodes:, :] = side_ref[...]


def tile_kernel(place_ref, meta_ref, *refs):
    given, block_ref, out_ref, tiles, total, sems = refs[:4], refs[4], refs[5], refs[6], refs[7], refs[8]
    _, slots, size, _ = tiles.shape
    n_x = block_ref.shape[0]
    core, odd = place_ref[0], place_ref[1]

    def tile_copy(which, slot):
        return pltpu.make_async_copy(
            given[which].at[slot], tiles.at[which, slot], sems.at[which, slot]
        )

    def cell_of(which):
        cell_core, cell_odd = (core + which // 2) % 2, (odd + which % 2) % 2
        return cell_core, cell_odd, cell_core * 2 + cell_odd

    for which in range(4):

        def fetch(slot, carry):
            tile_copy(which, slot).start()
            return carry

        lax.fori_loop(0, meta_ref[cell_of(which)[2], 2, 0], fetch, 0)
    total[...] = jnp.zeros_like(total)
    for which in range(4):
        cell_core, cell_odd, cell = cell_of(which)

        def step(slot, carry):
            tile_copy(which, slot).wait()
            chip = meta_ref[cell, 1, slot]
            z, x = chip // n_x, lax.rem(chip, n_x)
            window = jnp.concatenate(
                [block_ref[x, z, cell_odd], block_ref[x, z, 2 + cell_odd]], axis=0
            )
            total[cell_core, meta_ref[cell, 0, slot]] += jnp.dot(
                tiles[which, slot], window, preferred_element_type=F32
            )
            return carry

        lax.fori_loop(0, meta_ref[cell, 2, 0], step, 0)
    for row in range(total.shape[1]):
        for cell_core in range(2):
            out_ref[row, cell_core] = total[cell_core, row].astype(BF16)


def add_kernel(parts_ref, out_ref):
    total = parts_ref[0].astype(F32)
    for part in range(1, parts_ref.shape[0]):
        total = total + parts_ref[part].astype(F32)
    out_ref[...] = total.astype(BF16)


def split_column(column):
    high = column.astype(BF16)
    low = (column - high.astype(F32)).astype(BF16)
    lane = lax.broadcasted_iota(jnp.int32, column.shape, 1)
    return jnp.where(lane == 0, high.astype(F32), jnp.where(lane == 1, low.astype(F32), 0.0)).astype(BF16)


def node_kernel(shares_ref, weight_ref, bias_ref, cot_ref, act_ref, grads_ref):
    width = weight_ref.shape[1]
    aggregated = jnp.concatenate([shares_ref[part] for part in range(shares_ref.shape[0])], axis=1)
    preact = jnp.dot(aggregated, weight_ref[...], preferred_element_type=F32) + bias_ref[...]
    sigmoid_part = jax.nn.sigmoid(preact)
    act_ref[...] = (preact * sigmoid_part).astype(BF16)
    grad = cot_ref[...].astype(F32) * sigmoid_part * (1.0 + preact * (1.0 - sigmoid_part))
    rounded = grad.astype(BF16)
    rest = (grad - rounded.astype(F32)).astype(BF16)
    over_nodes = (((0,), (0,)), ((), ()))
    grads_ref[:, :width] = lax.dot_general(
        aggregated, rounded, over_nodes, preferred_element_type=F32
    ).astype(BF16)
    ones = jnp.ones((grad.shape[0], LANES), BF16)
    column = lax.dot_general(rounded, ones, over_nodes, preferred_element_type=F32)
    column = column + lax.dot_general(rest, ones, over_nodes, preferred_element_type=F32)
    grads_ref[:, width:] = split_column(column)


def sum_kernel(parts_ref, out_ref):
    width = parts_ref.shape[2] - LANES
    total = parts_ref[0].astype(F32)
    for part in range(1, parts_ref.shape[0]):
        total = total + parts_ref[part].astype(F32)
    main = total[:, :width].astype(BF16)
    column = total[:, width : width + 1] + total[:, width + 1 : width + 2]
    side = split_column(jnp.broadcast_to(column, (column.shape[0], LANES)))
    for copy in range(out_ref.shape[0]):
        out_ref[copy, :, :width] = main
        out_ref[copy, :, width:] = side


def sum_parts(parts, copies):
    return pl.pallas_call(
        sum_kernel,
        out_shape=jax.ShapeDtypeStruct((copies,) + parts.shape[1:], BF16),
        in_specs=[VMEM],
        out_specs=VMEM,
        compiler_params=PARAMS,
    )(parts)


def last_kernel(parts_ref, weight_ref, bias_ref):
    width = weight_ref.shape[1]
    weight_ref[...] = parts_ref[:, :width].astype(F32)
    side = jnp.transpose(parts_ref[:, width:].astype(F32))
    bias_ref[...] = side[0:1] + side[1:2]


def call(kernel, out, *args):
    shapes = jax.tree.map(lambda o: jax.ShapeDtypeStruct(*o), out, is_leaf=lambda o: isinstance(o[0], tuple) and not isinstance(o[1], tuple))
    specs = jax.tree.map(lambda o: VMEM, shapes)
    return pl.pallas_call(
        kernel, out_shape=shapes, in_specs=[VMEM] * len(args), out_specs=specs, compiler_params=PARAMS
    )(*args)


def swap(array, axis):
    return lax.ppermute(array, axis, [(0, 1), (1, 0)])


def per_device(
    features, weight, bias_term, cotangent, tile_values, tile_rows, tile_cols, tile_count
):
    nodes, width = features.shape
    _, _, slots, size, _ = tile_values.shape
    n_z, n_x = lax.axis_size("z_lo"), lax.axis_size("x")
    n_rest = lax.axis_size(REST)
    tiles = tile_values[0, 0]
    ints = [tile_rows[0, 0], tile_cols[0, 0], jnp.broadcast_to(tile_count[0], (slots,))]
    side = jnp.pad(jnp.stack(ints), ((0, SIDE - 3), (0, LANES - slots))).astype(BF16)
    quarters = call(quarter_kernel, ((4, nodes + SIDE, LANES), BF16), features, side)
    quarters = lax.all_to_all(quarters, QUAD, 0, 0)
    quarters, tiles = lax.optimization_barrier((quarters, tiles))
    tiles_y = swap(tiles, "y_odd")
    tiles_core = swap(tiles, "core")
    tiles_both = swap(tiles_y, "core")
    meta = quarters[:, nodes : nodes + 3, :slots].astype(jnp.int32)
    near = lax.all_gather(quarters[:, :nodes], "z_lo", axis=0)
    blocks = lax.all_to_all(jnp.broadcast_to(near[None], (n_x,) + near.shape), "x", 0, 0)
    place = jnp.stack([lax.axis_index(axis) for axis in QUAD]).astype(jnp.int32)
    term = pl.pallas_call(
        tile_kernel,
        out_shape=jax.ShapeDtypeStruct((n_rest, 2, size, LANES), BF16),
        in_specs=[SMEM, SMEM] + [ANY] * 4 + [VMEM],
        out_specs=VMEM,
        scratch_shapes=[
            pltpu.VMEM((4, slots, size, size), BF16),
            pltpu.VMEM((2, n_rest, size, LANES), F32),
            pltpu.SemaphoreType.DMA((4, slots)),
        ],
        compiler_params=PARAMS,
    )(place, meta, tiles, tiles_y, tiles_core, tiles_both, blocks)
    shares = lax.all_to_all(term, REST, 0, 0)
    shares = call(add_kernel, ((2, size, LANES), BF16), shares)
    shares = lax.all_to_all(shares.reshape(4, nodes, LANES), QUAD, 0, 0)
    activations, grads = call(
        node_kernel,
        (((nodes, width), BF16), ((width, width + LANES), BF16)),
        shares,
        weight,
        bias_term[None, :],
        cotangent,
    )
    n_plane, n_depth = lax.axis_size(PLANE), lax.axis_size(DEPTH)
    wide = width + LANES
    grads = sum_parts(lax.all_to_all(grads.reshape(4, width // 4, wide), QUAD, 0, 0), 1)
    grads = grads.reshape(n_plane, width // 4 // n_plane, wide)
    grads = sum_parts(lax.all_to_all(grads, PLANE, 0, 0), n_depth)
    grads = sum_parts(lax.all_to_all(grads, DEPTH, 0, 0), n_plane)
    grads = lax.all_to_all(grads, PLANE, 0, 0).reshape(1, width // 4, wide)
    grads = lax.all_to_all(jnp.broadcast_to(grads, (4,) + grads.shape[1:]), QUAD, 0, 0)
    weight_grad, bias_grad = call(
        last_kernel,
        (((width, width), F32), ((1, width), F32)),
        grads.reshape(width, wide),
    )
    return activations, weight_grad, bias_grad[0]


def solution(mesh):
    cut = Mesh(mesh.devices.reshape(SIZES), AXES)
    everywhere = P(AXES, None)
    return jax.shard_map(
        per_device,
        mesh=cut,
        in_specs=(
            everywhere,
            P(),
            P(),
            everywhere,
            P(ROW, COL, None, None, None),
            P(ROW, COL, None),
            P(ROW, COL, None),
            P(ROW, COL),
        ),
        out_specs=(everywhere, P(), P()),
        check_vma=False,
    )
```

```python
import jax
import jax.numpy as jnp
from jax import lax
from jax.experimental import pallas as pl
from jax.experimental.pallas import tpu as pltpu
from jax.sharding import Mesh, PartitionSpec as P

F32 = jnp.float32
BF16 = jnp.bfloat16
LANES = 128
VMEM = pl.BlockSpec(memory_space=pltpu.VMEM)
SMEM = pl.BlockSpec(memory_space=pltpu.SMEM)
ANY = pl.BlockSpec(memory_space=pl.ANY)
PARAMS = pltpu.CompilerParams(vmem_limit_bytes=40 * 1024 * 1024)
AXES = ("z_lo", "x", "core", "z_hi", "y_pair", "y_odd")
ROW = ("z_lo", "x", "core")
COL = ("z_hi", "y_pair", "y_odd")
QUAD = ("core", "y_odd")
PLANE = ("x", "y_pair")
DEPTH = ("z_lo", "z_hi")
SIZES = (4, 4, 2, 2, 4, 2)
SIDE = 16


def quarter_kernel(features_ref, cot_ref, side_ref, out_ref):
    nodes = features_ref.shape[0]
    for part in range(out_ref.shape[0]):
        lanes = slice(part * LANES, (part + 1) * LANES)
        out_ref[part, :nodes, :] = features_ref[:, lanes]
        out_ref[part, nodes : 2 * nodes, :] = cot_ref[:, lanes]
        out_ref[part, 2 * nodes :, :] = side_ref[...]


def tile_kernel(place_ref, meta_ref, *refs):
    given, block_ref, out_ref, tiles, total, sems = refs[:4], refs[4], refs[5], refs[6], refs[7], refs[8]
    _, slots, size, _ = tiles.shape
    n_x = block_ref.shape[0]
    core, odd = place_ref[0], place_ref[1]

    def tile_copy(which, slot):
        return pltpu.make_async_copy(
            given[which].at[slot], tiles.at[which, slot], sems.at[which, slot]
        )

    def cell_of(which):
        cell_core, cell_odd = (core + which // 2) % 2, (odd + which % 2) % 2
        return cell_core, cell_odd, cell_core * 2 + cell_odd

    for which in range(4):

        def fetch(slot, carry):
            tile_copy(which, slot).start()
            return carry

        lax.fori_loop(0, meta_ref[cell_of(which)[2], 2, 0], fetch, 0)
    total[...] = jnp.zeros_like(total)
    for which in range(4):
        cell_core, cell_odd, cell = cell_of(which)

        def step(slot, carry):
            tile_copy(which, slot).wait()
            chip = meta_ref[cell, 1, slot]
            z, x = chip // n_x, lax.rem(chip, n_x)
            window = jnp.concatenate(
                [block_ref[x, z, cell_odd], block_ref[x, z, 2 + cell_odd]], axis=0
            )
            total[cell_core, meta_ref[cell, 0, slot]] += jnp.dot(
                tiles[which, slot], window, preferred_element_type=F32
            )
            return carry

        lax.fori_loop(0, meta_ref[cell, 2, 0], step, 0)
    n_pair = out_ref.shape[0]
    for row in range(total.shape[1]):
        for cell_core in range(2):
            out_ref[row % n_pair, row // n_pair, cell_core] = total[cell_core, row].astype(BF16)


def add(ref):
    total = ref[0].astype(F32)
    for part in range(1, ref.shape[0]):
        total = total + ref[part].astype(F32)
    return total


def pair_kernel(place_ref, parts_ref, keep_ref, send_ref):
    mine = place_ref[2]
    keep_ref[...] = add(parts_ref.at[:, mine])
    send_ref[...] = add(parts_ref.at[:, 1 - mine]).astype(BF16)


def spread_kernel(keep_ref, given_ref, out_ref):
    total = (keep_ref[...] + given_ref[...].astype(F32)).astype(BF16)
    for copy in range(out_ref.shape[0]):
        out_ref[copy] = total


def split_rows(row):
    high = row.astype(BF16)
    low = (row - high.astype(F32)).astype(BF16)
    tall = (SIDE, row.shape[1])
    place = lax.broadcasted_iota(jnp.int32, tall, 0)
    high = jnp.broadcast_to(high.astype(F32), tall)
    low = jnp.broadcast_to(low.astype(F32), tall)
    return jnp.where(place == 0, high, jnp.where(place == 1, low, 0.0)).astype(BF16)


def node_kernel(place_ref, shares_ref, quarters_ref, weight_ref, bias_ref, act_ref, grads_ref):
    quad, nodes = shares_ref.shape[0], shares_ref.shape[2]
    me = place_ref[0] * 2 + place_ref[1]
    aggregated = jnp.concatenate(
        [
            jnp.concatenate([shares_ref[part, group] for part in range(quad)], axis=1)
            for group in range(quad)
        ],
        axis=0,
    )
    own = jnp.concatenate([shares_ref[part, me] for part in range(quad)], axis=1)
    preact = jnp.dot(own, weight_ref[...], preferred_element_type=F32) + bias_ref[...]
    act_ref[...] = (preact * jax.nn.sigmoid(preact)).astype(BF16)
    lanes = pl.ds(pl.multiple_of(me * LANES, LANES), LANES)
    preact = jnp.dot(aggregated, weight_ref[:, lanes], preferred_element_type=F32) + bias_ref[:, lanes]
    sigmoid_part = jax.nn.sigmoid(preact)
    cot = jnp.concatenate([quarters_ref[group, nodes : 2 * nodes] for group in range(quad)], axis=0)
    grad = cot.astype(F32) * sigmoid_part * (1.0 + preact * (1.0 - sigmoid_part))
    product = lax.dot_general(
        aggregated, grad.astype(BF16), (((0,), (0,)), ((), ())), preferred_element_type=F32
    ).astype(BF16)
    side = split_rows(jnp.sum(grad, axis=0, keepdims=True))
    n_chunks, tall, _ = grads_ref.shape
    depth = tall - SIDE
    for chunk in range(n_chunks):
        grads_ref[chunk, :depth] = product[chunk * depth : (chunk + 1) * depth]
        grads_ref[chunk, depth:] = side


def sum_kernel(parts_ref, out_ref):
    total = add(parts_ref)
    depth = total.shape[0] - SIDE
    main = total[:depth].astype(BF16)
    side = split_rows(total[depth : depth + 1] + total[depth + 1 : depth + 2])
    for copy in range(out_ref.shape[0]):
        out_ref[copy, :depth] = main
        out_ref[copy, depth:] = side


def copy_kernel(given_ref, out_ref):
    n_chunks, tall, _ = given_ref.shape
    depth = tall - SIDE
    for copy in range(out_ref.shape[0]):
        for chunk in range(n_chunks):
            out_ref[copy, chunk * depth : (chunk + 1) * depth] = given_ref[chunk, :depth]
        out_ref[copy, n_chunks * depth :] = given_ref[0, depth:]


def last_kernel(parts_ref, weight_ref, bias_ref):
    width = weight_ref.shape[0]
    for part in range(parts_ref.shape[0]):
        lanes = slice(part * LANES, (part + 1) * LANES)
        weight_ref[:, lanes] = parts_ref[part, :width].astype(F32)
        side = parts_ref[part, width:].astype(F32)
        bias_ref[:, lanes] = side[0:1] + side[1:2]


def call(kernel, out, *args, scalars=0):
    shapes = jax.tree.map(lambda o: jax.ShapeDtypeStruct(*o), out, is_leaf=lambda o: isinstance(o[0], tuple) and not isinstance(o[1], tuple))
    specs = jax.tree.map(lambda o: VMEM, shapes)
    return pl.pallas_call(
        kernel, out_shape=shapes, in_specs=[SMEM] * scalars + [VMEM] * (len(args) - scalars), out_specs=specs, compiler_params=PARAMS
    )(*args)


def swap(array, axis):
    return lax.ppermute(array, axis, [(0, 1), (1, 0)])


def per_device(
    features, weight, bias_term, cotangent, tile_values, tile_rows, tile_cols, tile_count
):
    nodes, width = features.shape
    _, _, slots, size, _ = tile_values.shape
    n_z, n_x = lax.axis_size("z_lo"), lax.axis_size("x")
    n_pair = lax.axis_size("y_pair")
    tiles = tile_values[0, 0]
    ints = [tile_rows[0, 0], tile_cols[0, 0], jnp.broadcast_to(tile_count[0], (slots,))]
    side = jnp.pad(jnp.stack(ints), ((0, SIDE - 3), (0, LANES - slots))).astype(BF16)
    quarters = call(
        quarter_kernel, ((4, 2 * nodes + SIDE, LANES), BF16), features, cotangent, side
    )
    quarters = lax.all_to_all(quarters, QUAD, 0, 0)
    quarters, tiles = lax.optimization_barrier((quarters, tiles))
    tiles_y = swap(tiles, "y_odd")
    tiles_core = swap(tiles, "core")
    tiles_both = swap(tiles_y, "core")
    meta = quarters[:, 2 * nodes : 2 * nodes + 3, :slots].astype(jnp.int32)
    near = lax.all_gather(quarters[:, :nodes], "z_lo", axis=0)
    blocks = lax.all_to_all(jnp.broadcast_to(near[None], (n_x,) + near.shape), "x", 0, 0)
    place = jnp.stack([lax.axis_index(axis) for axis in QUAD + ("z_hi",)]).astype(jnp.int32)
    term = pl.pallas_call(
        tile_kernel,
        out_shape=jax.ShapeDtypeStruct((n_pair, 2, 2, size, LANES), BF16),
        in_specs=[SMEM, SMEM] + [ANY] * 4 + [VMEM],
        out_specs=VMEM,
        scratch_shapes=[
            pltpu.VMEM((4, slots, size, size), BF16),
            pltpu.VMEM((2, 2 * n_pair, size, LANES), F32),
            pltpu.SemaphoreType.DMA((4, slots)),
        ],
        compiler_params=PARAMS,
    )(place, meta, tiles, tiles_y, tiles_core, tiles_both, blocks)
    shares = lax.all_to_all(term, "y_pair", 0, 0)
    block = (2, size, LANES)
    keep, send = call(pair_kernel, ((block, F32), (block, BF16)), place, shares, scalars=1)
    shares = call(spread_kernel, ((4,) + block, BF16), keep, swap(send, "z_hi"))
    shares = lax.all_to_all(shares.reshape(4, 4, nodes, LANES), QUAD, 0, 0)
    n_plane, n_depth = lax.axis_size(PLANE), lax.axis_size(DEPTH)
    chunk = (width // n_plane + SIDE, LANES)
    activations, grads = call(
        node_kernel,
        (((nodes, width), BF16), ((n_plane,) + chunk, BF16)),
        place,
        shares,
        quarters,
        weight,
        bias_term[None, :],
        scalars=1,
    )
    grads = lax.all_to_all(grads, PLANE, 0, 0)
    grads = call(sum_kernel, ((n_depth,) + chunk, BF16), grads)
    grads = lax.all_to_all(grads, DEPTH, 0, 0)
    grads = call(sum_kernel, ((n_plane,) + chunk, BF16), grads)
    grads = lax.all_to_all(grads, PLANE, 0, 0)
    grads = call(copy_kernel, ((4, width + SIDE, LANES), BF16), grads)
    grads = lax.all_to_all(grads, QUAD, 0, 0)
    weight_grad, bias_grad = call(
        last_kernel, (((width, width), F32), ((1, width), F32)), grads
    )
    return activations, weight_grad, bias_grad[0]


def solution(mesh):
    cut = Mesh(mesh.devices.reshape(SIZES), AXES)
    everywhere = P(AXES, None)
    return jax.shard_map(
        per_device,
        mesh=cut,
        in_specs=(
            everywhere,
            P(),
            P(),
            everywhere,
            P(ROW, COL, None, None, None),
            P(ROW, COL, None),
            P(ROW, COL, None),
            P(ROW, COL),
        ),
        out_specs=(everywhere, P(), P()),
        check_vma=False,
    )
```

```python
import jax
import jax.numpy as jnp
from jax import lax
from jax.experimental import pallas as pl
from jax.experimental.pallas import tpu as pltpu
from jax.sharding import Mesh, PartitionSpec as P

F32 = jnp.float32
BF16 = jnp.bfloat16
LANES = 128
VMEM = pl.BlockSpec(memory_space=pltpu.VMEM)
SMEM = pl.BlockSpec(memory_space=pltpu.SMEM)
HBM = pl.BlockSpec(memory_space=pltpu.HBM)
PARAMS = pltpu.CompilerParams(vmem_limit_bytes=40 * 1024 * 1024)
AXES = ("z_lo", "x", "core", "z_hi", "y_pair", "y_odd")
ROW = ("z_lo", "x", "core")
COL = ("z_hi", "y_pair", "y_odd")
QUAD = ("core", "y_odd")
FIRST = ("z_lo", "core", "y_odd")
DEPTH = ("z_lo", "z_hi")
Y = ("y_pair", "y_odd")
PLANE = ("x", "y_pair", "y_odd")
SIZES = (4, 4, 2, 2, 4, 2)
ROLES = ((0, 2, 5, 7), (1, 3, 4, 6))
PLANE_ROLES = tuple(tuple(x * 8 + y for x in range(4) for y in role) for role in ROLES)
SIDE = 16


def quarter_of(part, flip):
    return part // 2 * 2 + lax.rem(part % 2 + flip, 2)


def lanes_of(quarter):
    return pl.ds(pl.multiple_of(quarter * LANES, LANES), LANES)


def quarter_kernel(place_ref, rows_ref, cols_ref, count_ref, features_ref, out_ref, side, sems):
    nodes = features_ref.shape[0]
    copies = []
    for place in range(out_ref.shape[0]):
        lanes = lanes_of(quarter_of(place % 4, place_ref[3]))
        copies.append(
            pltpu.make_async_copy(
                features_ref.at[:, lanes], out_ref.at[place, pl.ds(0, nodes)], sems.at[0, place]
            )
        )
        copies[-1].start()
    row = lax.broadcasted_iota(jnp.int32, side.shape, 0)
    lane = lax.broadcasted_iota(jnp.int32, side.shape, 1)
    values = jnp.where(row == 2, count_ref[0], 0)
    for slot in range(rows_ref.shape[0]):
        for kind, ref in enumerate((rows_ref, cols_ref)):
            here = jnp.logical_and(row == kind, lane == slot)
            values = jnp.where(here, ref[slot], values)
    side[...] = values.astype(F32).astype(BF16)
    for place in range(out_ref.shape[0]):
        copies.append(
            pltpu.make_async_copy(
                side, out_ref.at[place, pl.ds(nodes, SIDE)], sems.at[1, place]
            )
        )
        copies[-1].start()
    for copy in copies:
        copy.wait()


def tile_kernel(place_ref, meta_ref, *refs):
    given, block_ref, out_ref, tiles, total, sems = refs[:4], refs[4], refs[5], refs[6], refs[7], refs[8]
    _, slots, size, _ = tiles.shape
    n_x = block_ref.shape[0]
    core, odd = place_ref[0], place_ref[1]

    def tile_copy(which, slot):
        return pltpu.make_async_copy(
            given[which].at[slot], tiles.at[which, slot], sems.at[which, slot]
        )

    def cell_of(which):
        cell_core, cell_odd = (core + which // 2) % 2, (odd + which % 2) % 2
        return cell_core, cell_odd, cell_core * 2 + cell_odd

    for which in range(4):

        def fetch(slot, carry):
            tile_copy(which, slot).start()
            return carry

        lax.fori_loop(0, meta_ref[cell_of(which)[2], 2, 0], fetch, 0)
    total[...] = jnp.zeros_like(total)
    for which in range(4):
        cell_core, cell_odd, cell = cell_of(which)

        def step(slot, carry):
            tile_copy(which, slot).wait()
            chip = meta_ref[cell, 1, slot]
            z, x = chip // n_x, lax.rem(chip, n_x)
            window = jnp.concatenate(
                [block_ref[x, z, cell_odd], block_ref[x, z, 2 + cell_odd]], axis=0
            )
            total[cell_core, meta_ref[cell, 0, slot]] += jnp.dot(
                tiles[which, slot], window, preferred_element_type=F32
            )
            return carry

        lax.fori_loop(0, meta_ref[cell, 2, 0], step, 0)
    n_pair = out_ref.shape[0]
    for row in range(total.shape[1]):
        for cell_core in range(2):
            out_ref[row % n_pair, row // n_pair, cell_core] = total[cell_core, row].astype(BF16)


def add(ref):
    total = ref[0].astype(F32)
    for part in range(1, ref.shape[0]):
        total = total + ref[part].astype(F32)
    return total


def pair_kernel(place_ref, parts_ref, keep_ref, send_ref):
    mine = place_ref[2]
    keep_ref[...] = add(parts_ref.at[:, mine])
    send_ref[...] = add(parts_ref.at[:, 1 - mine]).astype(BF16)


def spread_kernel(place_ref, keep_ref, given_ref, cot_ref, out_ref):
    total = (keep_ref[...] + given_ref[...].astype(F32)).astype(BF16)
    for part in range(out_ref.shape[0]):
        out_ref[part, : total.shape[0]] = total
        out_ref[part, total.shape[0]] = cot_ref[:, lanes_of(quarter_of(part, place_ref[3]))]


def split_rows(row):
    high = row.astype(BF16)
    low = (row - high.astype(F32)).astype(BF16)
    tall = (SIDE, row.shape[1])
    place = lax.broadcasted_iota(jnp.int32, tall, 0)
    high = jnp.broadcast_to(high.astype(F32), tall)
    low = jnp.broadcast_to(low.astype(F32), tall)
    return jnp.where(place == 0, high, jnp.where(place == 1, low, 0.0)).astype(BF16)


def node_kernel(place_ref, shares_ref, weight_ref, bias_ref, act_ref, grads_ref):
    quad = shares_ref.shape[0]
    me, flip = place_ref[0] * 2 + place_ref[1], place_ref[3]

    def rows_of(group):
        return jnp.concatenate(
            [shares_ref[quarter_of(part, flip), group] for part in range(quad)], axis=1
        )

    aggregated = jnp.concatenate([rows_of(group) for group in range(quad)], axis=0)
    preact = jnp.dot(rows_of(me), weight_ref[...], preferred_element_type=F32) + bias_ref[...]
    act_ref[...] = (preact * jax.nn.sigmoid(preact)).astype(BF16)
    lanes = lanes_of(quarter_of(me, flip))
    preact = jnp.dot(aggregated, weight_ref[:, lanes], preferred_element_type=F32) + bias_ref[:, lanes]
    sigmoid_part = jax.nn.sigmoid(preact)
    cot = jnp.concatenate([shares_ref[group, quad] for group in range(quad)], axis=0)
    grad = cot.astype(F32) * sigmoid_part * (1.0 + preact * (1.0 - sigmoid_part))
    product = lax.dot_general(
        aggregated, grad.astype(BF16), (((0,), (0,)), ((), ())), preferred_element_type=F32
    ).astype(BF16)
    side = split_rows(jnp.sum(grad, axis=0, keepdims=True))
    n_chunks, tall, _ = grads_ref.shape
    depth = tall - SIDE
    for chunk in range(n_chunks):
        grads_ref[chunk, :depth] = product[chunk * depth : (chunk + 1) * depth]
        grads_ref[chunk, depth:] = side


def sum_kernel(parts_ref, out_ref):
    total = add(parts_ref)
    depth = total.shape[0] - SIDE
    main = total[:depth].astype(BF16)
    side = split_rows(total[depth : depth + 1] + total[depth + 1 : depth + 2])
    for copy in range(out_ref.shape[0]):
        out_ref[copy, :depth] = main
        out_ref[copy, depth:] = side


def copy_kernel(given_ref, out_ref):
    n_chunks, tall, _ = given_ref.shape
    depth = tall - SIDE
    for copy in range(out_ref.shape[0]):
        for chunk in range(n_chunks):
            out_ref[copy, chunk * depth : (chunk + 1) * depth] = given_ref[chunk, :depth]
        out_ref[copy, n_chunks * depth :] = given_ref[0, depth:]


def last_kernel(place_ref, parts_ref, weight_ref, bias_ref):
    width = weight_ref.shape[0]
    for quarter in range(parts_ref.shape[0]):
        part = quarter_of(quarter, place_ref[3])
        lanes = slice(quarter * LANES, (quarter + 1) * LANES)
        weight_ref[:, lanes] = parts_ref[part, :width].astype(F32)
        side = parts_ref[part, width:].astype(F32)
        bias_ref[:, lanes] = side[0:1] + side[1:2]


def call(kernel, out, *args, scalars=0):
    shapes = jax.tree.map(lambda o: jax.ShapeDtypeStruct(*o), out, is_leaf=lambda o: isinstance(o[0], tuple) and not isinstance(o[1], tuple))
    specs = jax.tree.map(lambda o: VMEM, shapes)
    return pl.pallas_call(
        kernel, out_shape=shapes, in_specs=[SMEM] * scalars + [VMEM] * (len(args) - scalars), out_specs=specs, compiler_params=PARAMS
    )(*args)


def swap(array, axis):
    return lax.ppermute(array, axis, [(0, 1), (1, 0)])


def per_device(
    features, weight, bias_term, cotangent, tile_values, tile_rows, tile_cols, tile_count
):
    nodes, width = features.shape
    _, _, slots, size, _ = tile_values.shape
    n_x, n_pair = lax.axis_size("x"), lax.axis_size("y_pair")
    places = [lax.axis_index(axis) for axis in QUAD + ("z_hi",)]
    places.append(lax.axis_index("y_pair") // (n_pair // 2))
    place = jnp.stack(places).astype(jnp.int32)
    n_first = lax.axis_size(FIRST)
    quarters = pl.pallas_call(
        quarter_kernel,
        out_shape=jax.ShapeDtypeStruct((n_first, nodes + SIDE, LANES), BF16),
        in_specs=[SMEM] * 4 + [HBM],
        out_specs=HBM,
        scratch_shapes=[pltpu.VMEM((SIDE, LANES), BF16), pltpu.SemaphoreType.DMA((2, n_first))],
        compiler_params=PARAMS,
    )(place, tile_rows[0, 0], tile_cols[0, 0], tile_count[0], features)
    quarters = lax.all_to_all(quarters, FIRST, 0, 0)
    quarters, tiles = lax.optimization_barrier((quarters, tile_values[0, 0]))
    tiles_y = swap(tiles, "y_odd")
    tiles_core = swap(tiles, "core")
    tiles_both = swap(tiles_y, "core")
    quarters = quarters.reshape(-1, 4, nodes + SIDE, LANES)
    meta = lax.dynamic_index_in_dim(quarters, lax.axis_index("z_lo"), 0, keepdims=False)
    meta = meta[:, nodes : nodes + 3, :slots].astype(jnp.int32)
    near = quarters[:, :, :nodes]
    blocks = lax.all_to_all(jnp.broadcast_to(near[None], (n_x,) + near.shape), "x", 0, 0)
    term = pl.pallas_call(
        tile_kernel,
        out_shape=jax.ShapeDtypeStruct((n_pair, 2, 2, size, LANES), BF16),
        in_specs=[SMEM, SMEM] + [HBM] * 4 + [VMEM],
        out_specs=VMEM,
        scratch_shapes=[
            pltpu.VMEM((4, slots, size, size), BF16),
            pltpu.VMEM((2, 2 * n_pair, size, LANES), F32),
            pltpu.SemaphoreType.DMA((4, slots)),
        ],
        compiler_params=PARAMS,
    )(place, meta, tiles, tiles_y, tiles_core, tiles_both, blocks)
    shares = lax.all_to_all(term, Y, 0, 0, axis_index_groups=ROLES)
    block = (4, nodes, LANES)
    keep, send = call(
        pair_kernel,
        ((block, F32), (block, BF16)),
        place,
        shares.reshape((n_pair, 2) + block),
        scalars=1,
    )
    shares = call(
        spread_kernel,
        ((4, 5, nodes, LANES), BF16),
        place,
        keep,
        swap(send, "z_hi"),
        cotangent,
        scalars=1,
    )
    shares = lax.all_to_all(shares, QUAD, 0, 0)
    n_plane, n_depth = len(PLANE_ROLES[0]), lax.axis_size(DEPTH)
    chunk = (width // n_plane + SIDE, LANES)
    activations, grads = call(
        node_kernel,
        (((nodes, width), BF16), ((n_plane,) + chunk, BF16)),
        place,
        shares,
        weight,
        bias_term[None, :],
        scalars=1,
    )
    grads = lax.all_to_all(grads, PLANE, 0, 0, axis_index_groups=PLANE_ROLES)
    grads = call(sum_kernel, ((n_depth,) + chunk, BF16), grads)
    grads = lax.all_to_all(grads, DEPTH, 0, 0)
    grads = call(sum_kernel, ((n_plane,) + chunk, BF16), grads)
    grads = lax.all_to_all(grads, PLANE, 0, 0, axis_index_groups=PLANE_ROLES)
    grads = call(copy_kernel, ((4, width + SIDE, LANES), BF16), grads)
    grads = lax.all_to_all(grads, QUAD, 0, 0)
    weight_grad, bias_grad = call(
        last_kernel, (((width, width), F32), ((1, width), F32)), place, grads, scalars=1
    )
    return activations, weight_grad, bias_grad[0]


def solution(mesh):
    cut = Mesh(mesh.devices.reshape(SIZES), AXES)
    everywhere = P(AXES, None)
    return jax.shard_map(
        per_device,
        mesh=cut,
        in_specs=(
            everywhere,
            P(),
            P(),
            everywhere,
            P(ROW, COL, None, None, None),
            P(ROW, COL, None),
            P(ROW, COL, None),
            P(ROW, COL),
        ),
        out_specs=(everywhere, P(), P()),
        check_vma=False,
    )
```

```python
import jax
import jax.numpy as jnp
from jax import lax
from jax.experimental import pallas as pl
from jax.experimental.pallas import tpu as pltpu
from jax.sharding import Mesh, PartitionSpec as P

F32 = jnp.float32
BF16 = jnp.bfloat16
LANES = 128
VMEM = pl.BlockSpec(memory_space=pltpu.VMEM)
SMEM = pl.BlockSpec(memory_space=pltpu.SMEM)
HBM = pl.BlockSpec(memory_space=pltpu.HBM)
PARAMS = pltpu.CompilerParams(vmem_limit_bytes=40 * 1024 * 1024)
AXES = ("z_lo", "x", "core", "z_hi", "y_pair", "y_odd")
ROW = ("z_lo", "x", "core")
COL = ("z_hi", "y_pair", "y_odd")
QUAD = ("core", "y_odd")
PLANE = ("x", "y_pair")
DEPTH = ("z_lo", "z_hi", "core", "y_odd")
SIZES = (4, 4, 2, 2, 4, 2)
SIDE = 16
PAIR = 8


def lanes_of(part):
    return slice(part * LANES, (part + 1) * LANES)


def quarter_kernel(features_ref, side_ref, out_ref):
    nodes = features_ref.shape[0]
    for part in range(out_ref.shape[0]):
        out_ref[part, :nodes, :] = features_ref[:, lanes_of(part)]
        out_ref[part, nodes:, :] = side_ref[...]


def tile_kernel(place_ref, meta_ref, *refs):
    given, block_ref = refs[:4], refs[4]
    first_ref, keep_ref, send_ref, tiles, total, sems = refs[5:]
    _, slots, size, _ = tiles.shape
    n_x = block_ref.shape[0]
    core, odd = place_ref[0], place_ref[1]

    def tile_copy(which, slot):
        return pltpu.make_async_copy(
            given[which].at[slot], tiles.at[which, slot], sems.at[which, slot]
        )

    def cell_of(which):
        cell_core, cell_odd = (core + which // 2) % 2, (odd + which % 2) % 2
        return cell_core, cell_odd, cell_core * 2 + cell_odd

    for which in range(4):

        def fetch(slot, carry):
            tile_copy(which, slot).start()
            return carry

        lax.fori_loop(0, meta_ref[cell_of(which)[2], 2, 0], fetch, 0)
    total[...] = jnp.zeros_like(total)
    for which in range(4):
        cell_core, cell_odd, cell = cell_of(which)

        def step(slot, carry):
            tile_copy(which, slot).wait()
            chip = meta_ref[cell, 1, slot]
            z, x = chip // n_x, lax.rem(chip, n_x)
            window = jnp.concatenate(
                [block_ref[x, z, cell_odd], block_ref[x, z, 2 + cell_odd]], axis=0
            )
            total[cell_core, meta_ref[cell, 0, slot]] += jnp.dot(
                tiles[which, slot], window, preferred_element_type=F32
            )
            return carry

        lax.fori_loop(0, meta_ref[cell, 2, 0], step, 0)
    n_pair, mine = first_ref.shape[0], place_ref[2]
    for pair in range(n_pair):
        for high in range(2):
            first_ref[pair, high] = total[0, high * n_pair + pair].astype(BF16)
        keep_ref[pair] = total[1, mine * n_pair + pair]
        send_ref[pair] = total[1, (1 - mine) * n_pair + pair].astype(BF16)


def add(ref):
    total = ref[0].astype(F32)
    for part in range(1, ref.shape[0]):
        total = total + ref[part].astype(F32)
    return total


def pair_kernel(place_ref, parts_ref, keep_ref, send_ref):
    mine = place_ref[2]
    keep_ref[...] = add(parts_ref.at[:, mine])
    send_ref[...] = add(parts_ref.at[:, 1 - mine]).astype(BF16)


def join_kernel(keep_ref, given_ref, out_ref):
    out_ref[...] = (keep_ref[...] + given_ref[...].astype(F32)).astype(BF16)


def spread_kernel(keep_ref, given_ref, parts_ref, cot_ref, out_ref):
    nodes = cot_ref.shape[0]
    first = (keep_ref[...] + given_ref[...].astype(F32)).astype(BF16)
    second = add(parts_ref).astype(BF16)
    for part in range(out_ref.shape[0]):
        for half in range(2):
            out_ref[part, half] = first[half * nodes : (half + 1) * nodes]
            out_ref[part, 2 + half] = second[half * nodes : (half + 1) * nodes]
        out_ref[part, 4] = cot_ref[:, lanes_of(part)]


def split_rows(row):
    high = row.astype(BF16)
    low = (row - high.astype(F32)).astype(BF16)
    tall = (PAIR, row.shape[1])
    place = lax.broadcasted_iota(jnp.int32, tall, 0)
    high = jnp.broadcast_to(high.astype(F32), tall)
    low = jnp.broadcast_to(low.astype(F32), tall)
    return jnp.where(place == 0, high, jnp.where(place == 1, low, 0.0))


def node_kernel(place_ref, shares_ref, weight_ref, bias_ref, act_ref, grads_ref):
    quad = shares_ref.shape[0]
    me = place_ref[0] * 2 + place_ref[1]
    aggregated = jnp.concatenate(
        [
            jnp.concatenate([shares_ref[part, group] for part in range(quad)], axis=1)
            for group in range(quad)
        ],
        axis=0,
    )
    own = jnp.concatenate([shares_ref[part, me] for part in range(quad)], axis=1)
    preact = jnp.dot(own, weight_ref[...], preferred_element_type=F32) + bias_ref[...]
    act_ref[...] = (preact * jax.nn.sigmoid(preact)).astype(BF16)
    lanes = pl.ds(pl.multiple_of(me * LANES, LANES), LANES)
    preact = jnp.dot(aggregated, weight_ref[:, lanes], preferred_element_type=F32) + bias_ref[:, lanes]
    sigmoid_part = jax.nn.sigmoid(preact)
    cot = jnp.concatenate([shares_ref[group, quad] for group in range(quad)], axis=0)
    grad = cot.astype(F32) * sigmoid_part * (1.0 + preact * (1.0 - sigmoid_part))
    product = lax.dot_general(
        aggregated, grad.astype(BF16), (((0,), (0,)), ((), ())), preferred_element_type=F32
    ).astype(BF16)
    side = split_rows(jnp.sum(grad, axis=0, keepdims=True)).astype(BF16)
    n_chunks, tall, _ = grads_ref.shape
    depth = tall - PAIR
    for chunk in range(n_chunks):
        grads_ref[chunk, :depth] = product[chunk * depth : (chunk + 1) * depth]
        grads_ref[chunk, depth:] = side


def sum_kernel(parts_ref, out_ref):
    total = add(parts_ref)
    depth = total.shape[0] - PAIR
    main = total[:depth].astype(BF16)
    side = split_rows(total[depth : depth + 1] + total[depth + 1 : depth + 2]).astype(BF16)
    for copy in range(out_ref.shape[0]):
        out_ref[copy, :depth] = main
        out_ref[copy, depth:] = side


def depth_kernel(parts_ref, out_ref):
    n_z, quad, tall, lanes = parts_ref.shape
    depth = tall - PAIR
    place = lax.broadcasted_iota(jnp.int32, (PAIR, lanes), 0)
    side = jnp.zeros((PAIR, lanes), F32)
    mains = []
    for part in range(quad):
        total = parts_ref[0, part].astype(F32)
        for z in range(1, n_z):
            total = total + parts_ref[z, part].astype(F32)
        mains.append(total[:depth].astype(BF16))
        row = total[depth : depth + 1] + total[depth + 1 : depth + 2]
        high = row.astype(BF16).astype(F32)
        low = row - high
        high, low = (jnp.broadcast_to(part_row, side.shape) for part_row in (high, low))
        side = jnp.where(place == 2 * part, high, jnp.where(place == 2 * part + 1, low, side))
    side = side.astype(BF16)
    for copy in range(out_ref.shape[0]):
        for part in range(quad):
            out_ref[copy, part * depth : (part + 1) * depth] = mains[part]
        out_ref[copy, quad * depth :] = side


def last_kernel(parts_ref, weight_ref, bias_ref):
    n_chunks, tall, lanes = parts_ref.shape
    quad = weight_ref.shape[1] // lanes
    depth = (tall - PAIR) // quad
    for chunk in range(n_chunks):
        for part in range(quad):
            rows = slice(chunk * depth, (chunk + 1) * depth)
            weight_ref[rows, lanes_of(part)] = parts_ref[
                chunk, part * depth : (part + 1) * depth
            ].astype(F32)
    side = parts_ref[0, tall - PAIR :].astype(F32)
    for part in range(quad):
        bias_ref[:, lanes_of(part)] = side[2 * part : 2 * part + 1] + side[2 * part + 1 : 2 * part + 2]


def call(kernel, out, *args, scalars=0):
    shapes = jax.tree.map(lambda o: jax.ShapeDtypeStruct(*o), out, is_leaf=lambda o: isinstance(o[0], tuple) and not isinstance(o[1], tuple))
    specs = jax.tree.map(lambda o: VMEM, shapes)
    return pl.pallas_call(
        kernel, out_shape=shapes, in_specs=[SMEM] * scalars + [VMEM] * (len(args) - scalars), out_specs=specs, compiler_params=PARAMS
    )(*args)


def swap(array, axis):
    return lax.ppermute(array, axis, [(0, 1), (1, 0)])


def per_device(
    features, weight, bias_term, cotangent, tile_values, tile_rows, tile_cols, tile_count
):
    nodes, width = features.shape
    _, _, slots, size, _ = tile_values.shape
    n_z, n_x = lax.axis_size("z_lo"), lax.axis_size("x")
    n_pair = lax.axis_size("y_pair")
    tiles = tile_values[0, 0]
    ints = [tile_rows[0, 0], tile_cols[0, 0], jnp.broadcast_to(tile_count[0], (slots,))]
    side = jnp.pad(jnp.stack(ints), ((0, SIDE - 3), (0, LANES - slots))).astype(BF16)
    quarters = call(quarter_kernel, ((4, nodes + SIDE, LANES), BF16), features, side)
    quarters = lax.all_to_all(quarters, QUAD, 0, 0)
    quarters, tiles = lax.optimization_barrier((quarters, tiles))
    tiles_y = swap(tiles, "y_odd")
    tiles_core = swap(tiles, "core")
    tiles_both = swap(tiles_y, "core")
    meta = quarters[:, nodes : nodes + 3, :slots].astype(jnp.int32)
    near = lax.all_gather(quarters[:, :nodes], "z_lo", axis=0)
    blocks = lax.all_to_all(jnp.broadcast_to(near[None], (n_x,) + near.shape), "x", 0, 0)
    place = jnp.stack([lax.axis_index(axis) for axis in QUAD + ("z_hi",)]).astype(jnp.int32)
    block = (size, LANES)
    first, keep, send = pl.pallas_call(
        tile_kernel,
        out_shape=(
            jax.ShapeDtypeStruct((n_pair, 2) + block, BF16),
            jax.ShapeDtypeStruct((n_pair,) + block, F32),
            jax.ShapeDtypeStruct((n_pair,) + block, BF16),
        ),
        in_specs=[SMEM, SMEM] + [HBM] * 4 + [VMEM],
        out_specs=(VMEM, VMEM, VMEM),
        scratch_shapes=[
            pltpu.VMEM((4, slots, size, size), BF16),
            pltpu.VMEM((2, 2 * n_pair) + block, F32),
            pltpu.SemaphoreType.DMA((4, slots)),
        ],
        compiler_params=PARAMS,
    )(place, meta, tiles, tiles_y, tiles_core, tiles_both, blocks)
    first = lax.all_to_all(first, "y_pair", 0, 0)
    second = call(join_kernel, ((n_pair,) + block, BF16), keep, swap(send, "z_hi"))
    second = lax.all_to_all(second, "y_pair", 0, 0)
    keep, send = call(pair_kernel, ((block, F32), (block, BF16)), place, first, scalars=1)
    shares = call(
        spread_kernel, ((4, 5, nodes, LANES), BF16), keep, swap(send, "z_hi"), second, cotangent
    )
    shares = lax.all_to_all(shares, QUAD, 0, 0)
    n_plane, n_depth = lax.axis_size(PLANE), lax.axis_size(DEPTH)
    depth = width // n_plane
    activations, grads = call(
        node_kernel,
        (((nodes, width), BF16), ((n_plane, depth + PAIR, LANES), BF16)),
        place,
        shares,
        weight,
        bias_term[None, :],
        scalars=1,
    )
    grads = lax.all_to_all(grads, PLANE, 0, 0)
    grads = call(sum_kernel, ((n_depth, depth + PAIR, LANES), BF16), grads)
    grads = lax.all_to_all(grads, DEPTH, 0, 0).reshape(-1, 4, depth + PAIR, LANES)
    grads = call(depth_kernel, ((n_plane, 4 * depth + PAIR, LANES), BF16), grads)
    grads = lax.all_to_all(grads, PLANE, 0, 0)
    weight_grad, bias_grad = call(
        last_kernel, (((width, width), F32), ((1, width), F32)), grads
    )
    return activations, weight_grad, bias_grad[0]


def solution(mesh):
    cut = Mesh(mesh.devices.reshape(SIZES), AXES)
    everywhere = P(AXES, None)
    return jax.shard_map(
        per_device,
        mesh=cut,
        in_specs=(
            everywhere,
            P(),
            P(),
            everywhere,
            P(ROW, COL, None, None, None),
            P(ROW, COL, None),
            P(ROW, COL, None),
            P(ROW, COL),
        ),
        out_specs=(everywhere, P(), P()),
        check_vma=False,
    )
```

```python
import jax
import jax.numpy as jnp
from jax import lax
from jax.experimental import pallas as pl
from jax.experimental.pallas import tpu as pltpu
from jax.sharding import Mesh, PartitionSpec as P

F32 = jnp.float32
BF16 = jnp.bfloat16
LANES = 128
VMEM = pl.BlockSpec(memory_space=pltpu.VMEM)
SMEM = pl.BlockSpec(memory_space=pltpu.SMEM)
HBM = pl.BlockSpec(memory_space=pltpu.HBM)
PARAMS = pltpu.CompilerParams(vmem_limit_bytes=40 * 1024 * 1024)
AXES = ("z_lo", "x", "core", "z_hi", "y_pair", "y_odd")
ROW = ("z_lo", "x", "core")
COL = ("z_hi", "y_pair", "y_odd")
QUAD = ("core", "y_odd")
HOME = ("core", "z_hi", "y_pair", "y_odd")
NEAR = ("x", "core")
Y = ("y_pair", "y_odd")
Z = ("z_lo", "z_hi")
SIZES = (4, 4, 2, 2, 4, 2)
SIDE = 16
PAIR = 8


def lanes_of(part):
    return slice(part * LANES, (part + 1) * LANES)


def quarter_kernel(features_ref, side_ref, out_ref):
    nodes = features_ref.shape[0]
    for part in range(out_ref.shape[0]):
        out_ref[part, :nodes, :] = features_ref[:, lanes_of(part)]
        out_ref[part, nodes:, :] = side_ref[...]


def tile_kernel(place_ref, meta_ref, *refs):
    given, block_ref, out_ref, tiles, total, sems = refs[:4], refs[4], refs[5], refs[6], refs[7], refs[8]
    _, slots, size, _ = tiles.shape
    n_x = block_ref.shape[0]
    core, odd = place_ref[0], place_ref[1]

    def tile_copy(which, slot):
        return pltpu.make_async_copy(
            given[which].at[slot], tiles.at[which, slot], sems.at[which, slot]
        )

    def cell_of(which):
        cell_core, cell_odd = (core + which // 2) % 2, (odd + which % 2) % 2
        return cell_core, cell_odd, cell_core * 2 + cell_odd

    for which in range(4):

        def fetch(slot, carry):
            tile_copy(which, slot).start()
            return carry

        lax.fori_loop(0, meta_ref[cell_of(which)[2], 2, 0], fetch, 0)
    total[...] = jnp.zeros_like(total)
    for which in range(4):
        cell_core, cell_odd, cell = cell_of(which)

        def step(slot, carry):
            tile_copy(which, slot).wait()
            chip = meta_ref[cell, 1, slot]
            z, x = chip // n_x, lax.rem(chip, n_x)
            window = jnp.concatenate(
                [block_ref[x, z, cell_odd], block_ref[x, z, 2 + cell_odd]], axis=0
            )
            total[cell_core, meta_ref[cell, 0, slot]] += jnp.dot(
                tiles[which, slot], window, preferred_element_type=F32
            )
            return carry

        lax.fori_loop(0, meta_ref[cell, 2, 0], step, 0)
    out_ref[...] = total[...].astype(BF16)


def add(ref):
    total = ref[0].astype(F32)
    for part in range(1, ref.shape[0]):
        total = total + ref[part].astype(F32)
    return total


def with_bias(main, row):
    high = row.astype(BF16).astype(F32)
    tall = (PAIR, row.shape[1])
    place = lax.broadcasted_iota(jnp.int32, tall, 0)
    high, low = (jnp.broadcast_to(part, tall) for part in (high, row - high))
    side = jnp.where(place == 0, high, jnp.where(place == 1, low, 0.0))
    return jnp.concatenate([main, side], axis=0).astype(BF16)


def bias_of(total):
    depth = total.shape[0] - PAIR
    return total[depth : depth + 1] + total[depth + 1 : depth + 2]


def node_kernel(parts_ref, weight_ref, bias_ref, cot_ref, act_ref, grads_ref):
    n_high, n_odd = parts_ref.shape[1], parts_ref.shape[2]
    quarters = []
    for core in range(parts_ref.shape[0]):
        for odd in range(n_odd):
            total = parts_ref[core, 0, odd].astype(F32)
            for high in range(1, n_high):
                total = total + parts_ref[core, high, odd].astype(F32)
            quarters.append(total.astype(BF16))
    aggregated = jnp.concatenate(quarters, axis=1)
    preact = jnp.dot(aggregated, weight_ref[...], preferred_element_type=F32) + bias_ref[...]
    sigmoid_part = jax.nn.sigmoid(preact)
    act_ref[...] = (preact * sigmoid_part).astype(BF16)
    grad = cot_ref[...].astype(F32) * sigmoid_part * (1.0 + preact * (1.0 - sigmoid_part))
    product = lax.dot_general(
        aggregated, grad.astype(BF16), (((0,), (0,)), ((), ())), preferred_element_type=F32
    )
    row = jnp.sum(grad, axis=0, keepdims=True)
    depth = grads_ref.shape[1] - PAIR
    for chunk in range(grads_ref.shape[0]):
        grads_ref[chunk] = with_bias(product[chunk * depth : (chunk + 1) * depth], row)


def scatter_kernel(parts_ref, out_ref):
    total = add(parts_ref)
    depth = out_ref.shape[1] - PAIR
    for chunk in range(out_ref.shape[0]):
        out_ref[chunk] = with_bias(total[chunk * depth : (chunk + 1) * depth], bias_of(total))


def sum_kernel(parts_ref, out_ref):
    total = add(parts_ref)
    rounded = with_bias(total[: total.shape[0] - PAIR], bias_of(total))
    for copy in range(out_ref.shape[0]):
        out_ref[copy] = rounded


def copy_kernel(parts_ref, out_ref):
    depth = parts_ref.shape[1] - PAIR
    parts = [parts_ref[part].astype(F32) for part in range(parts_ref.shape[0])]
    rows = jnp.concatenate([part[:depth] for part in parts] + [parts[0][depth:]], axis=0).astype(BF16)
    for copy in range(out_ref.shape[0]):
        out_ref[copy] = rows


def last_kernel(parts_ref, weight_ref, bias_ref):
    depth = parts_ref.shape[1] - PAIR
    for chunk in range(parts_ref.shape[0]):
        rows = parts_ref[chunk].astype(F32)
        weight_ref[chunk * depth : (chunk + 1) * depth] = rows[:depth]
        if chunk == 0:
            bias_ref[...] = bias_of(rows)


def call(kernel, out, *args, scalars=0):
    shapes = jax.tree.map(lambda o: jax.ShapeDtypeStruct(*o), out, is_leaf=lambda o: isinstance(o[0], tuple) and not isinstance(o[1], tuple))
    specs = jax.tree.map(lambda o: VMEM, shapes)
    return pl.pallas_call(
        kernel, out_shape=shapes, in_specs=[SMEM] * scalars + [VMEM] * (len(args) - scalars), out_specs=specs, compiler_params=PARAMS
    )(*args)


def swap(array, axis):
    return lax.ppermute(array, axis, [(0, 1), (1, 0)])


def per_device(
    features, weight, bias_term, cotangent, tile_values, tile_rows, tile_cols, tile_count
):
    nodes, width = features.shape
    _, _, slots, size, _ = tile_values.shape
    n_z, n_x = lax.axis_size("z_lo"), lax.axis_size("x")
    n_pair = lax.axis_size("y_pair")
    tiles = tile_values[0, 0]
    ints = [tile_rows[0, 0], tile_cols[0, 0], jnp.broadcast_to(tile_count[0], (slots,))]
    side = jnp.pad(jnp.stack(ints), ((0, SIDE - 3), (0, LANES - slots))).astype(BF16)
    quarters = call(quarter_kernel, ((4, nodes + SIDE, LANES), BF16), features, side)
    quarters = lax.all_to_all(quarters, QUAD, 0, 0)
    quarters, tiles = lax.optimization_barrier((quarters, tiles))
    tiles_y = swap(tiles, "y_odd")
    tiles_core = swap(tiles, "core")
    tiles_both = swap(tiles_y, "core")
    meta = quarters[:, nodes : nodes + 3, :slots].astype(jnp.int32)
    near = lax.all_gather(quarters[:, :nodes], "z_lo", axis=0)
    blocks = lax.all_to_all(jnp.broadcast_to(near[None], (n_x,) + near.shape), "x", 0, 0)
    place = jnp.stack([lax.axis_index(axis) for axis in QUAD]).astype(jnp.int32)
    term = pl.pallas_call(
        tile_kernel,
        out_shape=jax.ShapeDtypeStruct((2, 2 * n_pair, size, LANES), BF16),
        in_specs=[SMEM, SMEM] + [HBM] * 4 + [VMEM],
        out_specs=VMEM,
        scratch_shapes=[
            pltpu.VMEM((4, slots, size, size), BF16),
            pltpu.VMEM((2, 2 * n_pair, size, LANES), F32),
            pltpu.SemaphoreType.DMA((4, slots)),
        ],
        compiler_params=PARAMS,
    )(place, meta, tiles, tiles_y, tiles_core, tiles_both, blocks)
    shares = lax.all_to_all(term.reshape(-1, nodes, LANES), HOME, 0, 0)
    n_near, n_y, n_deep = lax.axis_size(NEAR), lax.axis_size(Y), lax.axis_size(Z)
    depth = width // n_near
    tall, short = depth + PAIR, depth // n_y + PAIR
    activations, grads = call(
        node_kernel,
        (((nodes, width), BF16), ((n_near, tall, width), BF16)),
        shares.reshape(2, 2 * n_pair, 2, nodes, LANES),
        weight,
        bias_term[None, :],
        cotangent,
    )
    grads = lax.all_to_all(grads, NEAR, 0, 0)
    grads = call(scatter_kernel, ((n_y, short, width), BF16), grads)
    grads = lax.all_to_all(grads, Y, 0, 0)
    grads = call(sum_kernel, ((n_deep, short, width), BF16), grads)
    grads = lax.all_to_all(grads, Z, 0, 0)
    grads = call(sum_kernel, ((n_y, short, width), BF16), grads)
    grads = lax.all_to_all(grads, Y, 0, 0)
    grads = call(copy_kernel, ((n_near, tall, width), BF16), grads)
    grads = lax.all_to_all(grads, NEAR, 0, 0)
    weight_grad, bias_grad = call(
        last_kernel, (((width, width), F32), ((1, width), F32)), grads
    )
    return activations, weight_grad, bias_grad[0]


def solution(mesh):
    cut = Mesh(mesh.devices.reshape(SIZES), AXES)
    everywhere = P(AXES, None)
    return jax.shard_map(
        per_device,
        mesh=cut,
        in_specs=(
            everywhere,
            P(),
            P(),
            everywhere,
            P(ROW, COL, None, None, None),
            P(ROW, COL, None),
            P(ROW, COL, None),
            P(ROW, COL),
        ),
        out_specs=(everywhere, P(), P()),
        check_vma=False,
    )
```

```python
import jax
import jax.numpy as jnp
from jax import lax
from jax.experimental import pallas as pl
from jax.experimental.pallas import tpu as pltpu
from jax.sharding import Mesh, PartitionSpec as P

F32 = jnp.float32
BF16 = jnp.bfloat16
LANES = 128
VMEM = pl.BlockSpec(memory_space=pltpu.VMEM)
SMEM = pl.BlockSpec(memory_space=pltpu.SMEM)
HBM = pl.BlockSpec(memory_space=pltpu.HBM)
PARAMS = pltpu.CompilerParams(vmem_limit_bytes=40 * 1024 * 1024)
AXES = ("z_lo", "x", "core", "z_hi", "y_pair", "y_odd")
ROW = ("z_lo", "x", "core")
COL = ("z_hi", "y_pair", "y_odd")
QUAD = ("core", "y_odd")
HOME = ("core", "y_pair", "y_odd")
NEAR = ("x", "core")
Y = ("y_pair", "y_odd")
Z = ("z_lo", "z_hi")
SIZES = (4, 4, 2, 2, 4, 2)
SIDE = 16
PAIR = 8


def lanes_of(part):
    return slice(part * LANES, (part + 1) * LANES)


def quarter_kernel(features_ref, side_ref, out_ref):
    nodes = features_ref.shape[0]
    for part in range(out_ref.shape[0]):
        out_ref[part, :nodes, :] = features_ref[:, lanes_of(part)]
        out_ref[part, nodes:, :] = side_ref[...]


def tile_kernel(place_ref, meta_ref, *refs):
    given, block_ref, out_ref, tiles, total, sems = refs[:4], refs[4], refs[5], refs[6], refs[7], refs[8]
    _, slots, size, _ = tiles.shape
    n_x = block_ref.shape[0]
    core, odd = place_ref[0], place_ref[1]

    def tile_copy(which, slot):
        return pltpu.make_async_copy(
            given[which].at[slot], tiles.at[which, slot], sems.at[which, slot]
        )

    def cell_of(which):
        cell_core, cell_odd = (core + which // 2) % 2, (odd + which % 2) % 2
        return cell_core, cell_odd, cell_core * 2 + cell_odd

    for which in range(4):

        def fetch(slot, carry):
            tile_copy(which, slot).start()
            return carry

        lax.fori_loop(0, meta_ref[cell_of(which)[2], 2, 0], fetch, 0)
    total[...] = jnp.zeros_like(total)
    for which in range(4):
        cell_core, cell_odd, cell = cell_of(which)

        used = meta_ref[cell, 2, 0]

        def product(slot):
            chip = meta_ref[cell, 1, slot]
            z, x = chip // n_x, lax.rem(chip, n_x)
            window = jnp.concatenate(
                [block_ref[x, z, cell_odd], block_ref[x, z, 2 + cell_odd]], axis=0
            )
            return jnp.dot(tiles[which, slot], window, preferred_element_type=F32)

        def step(index, carry):
            slot = 2 * index
            both = slot + 1 < used
            other = jnp.where(both, slot + 1, slot)
            tile_copy(which, slot).wait()

            @pl.when(both)
            def _():
                tile_copy(which, other).wait()

            one, two = product(slot), product(other)
            total[cell_core, meta_ref[cell, 0, slot]] += one
            total[cell_core, meta_ref[cell, 0, other]] += jnp.where(both, two, 0.0)
            return carry

        lax.fori_loop(0, (used + 1) // 2, step, 0)
    n_pair, nodes = out_ref.shape[1], out_ref.shape[4]
    for cell_core in range(2):
        for pair in range(n_pair):
            for high in range(2):
                rows = total[cell_core, high * n_pair + pair].astype(BF16)
                for cell_odd in range(2):
                    out_ref[cell_core, pair, cell_odd, high] = rows[
                        cell_odd * nodes : (cell_odd + 1) * nodes
                    ]


def add(ref):
    total = ref[0].astype(F32)
    for part in range(1, ref.shape[0]):
        total = total + ref[part].astype(F32)
    return total


def repeat_kernel(given_ref, out_ref):
    for copy in range(out_ref.shape[0]):
        out_ref[copy] = given_ref[...]


def pair_kernel(place_ref, parts_ref, keep_ref, send_ref):
    mine = place_ref[2]
    for core in range(2):
        for odd in range(2):
            keep_ref[core * 2 + odd] = add(parts_ref.at[core, :, odd, mine])
            send_ref[core * 2 + odd] = add(parts_ref.at[core, :, odd, 1 - mine]).astype(BF16)


def with_bias(main, row):
    high = row.astype(BF16).astype(F32)
    tall = (PAIR, row.shape[1])
    place = lax.broadcasted_iota(jnp.int32, tall, 0)
    high, low = (jnp.broadcast_to(part, tall) for part in (high, row - high))
    side = jnp.where(place == 0, high, jnp.where(place == 1, low, 0.0))
    return jnp.concatenate([main, side], axis=0).astype(BF16)


def bias_of(total):
    depth = total.shape[0] - PAIR
    return total[depth : depth + 1] + total[depth + 1 : depth + 2]


def node_kernel(keep_ref, given_ref, weight_ref, bias_ref, cot_ref, act_ref, grads_ref):
    quarters = [
        (keep_ref[part] + given_ref[part].astype(F32)).astype(BF16)
        for part in range(keep_ref.shape[0])
    ]
    aggregated = jnp.concatenate(quarters, axis=1)
    preact = jnp.dot(aggregated, weight_ref[...], preferred_element_type=F32) + bias_ref[...]
    sigmoid_part = jax.nn.sigmoid(preact)
    act_ref[...] = (preact * sigmoid_part).astype(BF16)
    grad = cot_ref[...].astype(F32) * sigmoid_part * (1.0 + preact * (1.0 - sigmoid_part))
    product = lax.dot_general(
        aggregated, grad.astype(BF16), (((0,), (0,)), ((), ())), preferred_element_type=F32
    )
    row = jnp.sum(grad, axis=0, keepdims=True)
    depth = grads_ref.shape[1] - PAIR
    for chunk in range(grads_ref.shape[0]):
        grads_ref[chunk] = with_bias(product[chunk * depth : (chunk + 1) * depth], row)


def beside_bias(main, bias):
    high = bias.astype(BF16).astype(F32)
    side = jnp.concatenate([high, bias - high], axis=0)
    return jnp.concatenate([main, side], axis=1).astype(BF16)


def scatter_kernel(parts_ref, out_ref):
    total = add(parts_ref)
    depth, width = out_ref.shape[1], parts_ref.shape[2]
    row = bias_of(total)
    bias = jnp.concatenate([row[:, lanes_of(part)] for part in range(width // LANES)], axis=0)
    for chunk in range(out_ref.shape[0]):
        out_ref[chunk] = beside_bias(total[chunk * depth : (chunk + 1) * depth], bias)


def sum_kernel(parts_ref, out_ref):
    total = add(parts_ref)
    width = total.shape[1] - LANES
    side = total[:, width:]
    half = side.shape[0] // 2
    rounded = beside_bias(total[:, :width], side[:half] + side[half:])
    for copy in range(out_ref.shape[0]):
        out_ref[copy] = rounded


def copy_kernel(parts_ref, out_ref):
    width = out_ref.shape[2]
    parts = [parts_ref[part].astype(F32) for part in range(parts_ref.shape[0])]
    side = parts[0][:, width:]
    half = side.shape[0] // 2
    bias = side[:half] + side[half:]
    row = jnp.concatenate([bias[part : part + 1] for part in range(half)], axis=1)
    rows = with_bias(jnp.concatenate([part[:, :width] for part in parts], axis=0), row)
    for copy in range(out_ref.shape[0]):
        out_ref[copy] = rows


def last_kernel(parts_ref, weight_ref, bias_ref):
    depth = parts_ref.shape[1] - PAIR
    for chunk in range(parts_ref.shape[0]):
        rows = parts_ref[chunk].astype(F32)
        weight_ref[chunk * depth : (chunk + 1) * depth] = rows[:depth]
        if chunk == 0:
            bias_ref[...] = bias_of(rows)


def call(kernel, out, *args, scalars=0):
    shapes = jax.tree.map(lambda o: jax.ShapeDtypeStruct(*o), out, is_leaf=lambda o: isinstance(o[0], tuple) and not isinstance(o[1], tuple))
    specs = jax.tree.map(lambda o: VMEM, shapes)
    return pl.pallas_call(
        kernel, out_shape=shapes, in_specs=[SMEM] * scalars + [VMEM] * (len(args) - scalars), out_specs=specs, compiler_params=PARAMS
    )(*args)


def swap(array, axis):
    return lax.ppermute(array, axis, [(0, 1), (1, 0)])


def per_device(
    features, weight, bias_term, cotangent, tile_values, tile_rows, tile_cols, tile_count
):
    nodes, width = features.shape
    _, _, slots, size, _ = tile_values.shape
    n_z, n_x = lax.axis_size("z_lo"), lax.axis_size("x")
    n_pair = lax.axis_size("y_pair")
    tiles = tile_values[0, 0]
    ints = [tile_rows[0, 0], tile_cols[0, 0], jnp.broadcast_to(tile_count[0], (slots,))]
    side = jnp.pad(jnp.stack(ints), ((0, SIDE - 3), (0, LANES - slots))).astype(BF16)
    quarters = call(quarter_kernel, ((4, nodes + SIDE, LANES), BF16), features, side)
    quarters = lax.all_to_all(quarters, QUAD, 0, 0)
    quarters, tiles = lax.optimization_barrier((quarters, tiles))
    tiles_y = swap(tiles, "y_odd")
    tiles_core = swap(tiles, "core")
    tiles_both = swap(tiles_y, "core")
    meta = quarters[:, nodes : nodes + 3, :slots].astype(jnp.int32)
    near = lax.all_gather(quarters[:, :nodes], "z_lo", axis=0)
    near = call(repeat_kernel, ((n_x,) + near.shape, BF16), near)
    blocks = lax.all_to_all(near, "x", 0, 0)
    place = jnp.stack([lax.axis_index(axis) for axis in QUAD + ("z_hi",)]).astype(jnp.int32)
    term = pl.pallas_call(
        tile_kernel,
        out_shape=jax.ShapeDtypeStruct((2, n_pair, 2, 2, nodes, LANES), BF16),
        in_specs=[SMEM, SMEM] + [HBM] * 4 + [VMEM],
        out_specs=VMEM,
        scratch_shapes=[
            pltpu.VMEM((4, slots, size, size), BF16),
            pltpu.VMEM((2, 2 * n_pair, size, LANES), F32),
            pltpu.SemaphoreType.DMA((4, slots)),
        ],
        compiler_params=PARAMS,
    )(place, meta, tiles, tiles_y, tiles_core, tiles_both, blocks)
    shares = lax.all_to_all(term.reshape(-1, 2, nodes, LANES), HOME, 0, 0)
    block = (4, nodes, LANES)
    keep, send = call(
        pair_kernel,
        ((block, F32), (block, BF16)),
        place,
        shares.reshape(2, n_pair, 2, 2, nodes, LANES),
        scalars=1,
    )
    n_near, n_y, n_deep = lax.axis_size(NEAR), lax.axis_size(Y), lax.axis_size(Z)
    depth = width // n_near
    tall, wide = depth + PAIR, width + LANES
    activations, grads = call(
        node_kernel,
        (((nodes, width), BF16), ((n_near, tall, width), BF16)),
        keep,
        swap(send, "z_hi"),
        weight,
        bias_term[None, :],
        cotangent,
    )
    grads = lax.all_to_all(grads, NEAR, 0, 0)
    grads = call(scatter_kernel, ((n_y, depth // n_y, wide), BF16), grads)
    grads = lax.all_to_all(grads, Y, 0, 0)
    grads = call(sum_kernel, ((n_deep, depth // n_y, wide), BF16), grads)
    grads = lax.all_to_all(grads, Z, 0, 0)
    grads = call(sum_kernel, ((n_y, depth // n_y, wide), BF16), grads)
    grads = lax.all_to_all(grads, Y, 0, 0)
    grads = call(copy_kernel, ((n_near, tall, width), BF16), grads)
    grads = lax.all_to_all(grads, NEAR, 0, 0)
    weight_grad, bias_grad = call(
        last_kernel, (((width, width), F32), ((1, width), F32)), grads
    )
    return activations, weight_grad, bias_grad[0]


def solution(mesh):
    cut = Mesh(mesh.devices.reshape(SIZES), AXES)
    everywhere = P(AXES, None)
    return jax.shard_map(
        per_device,
        mesh=cut,
        in_specs=(
            everywhere,
            P(),
            P(),
            everywhere,
            P(ROW, COL, None, None, None),
            P(ROW, COL, None),
            P(ROW, COL, None),
            P(ROW, COL),
        ),
        out_specs=(everywhere, P(), P()),
        check_vma=False,
    )
```

```python
import jax
import jax.numpy as jnp
from jax import lax
from jax.experimental import pallas as pl
from jax.experimental.pallas import tpu as pltpu
from jax.sharding import Mesh, PartitionSpec as P

F32 = jnp.float32
BF16 = jnp.bfloat16
LANES = 128
VMEM = pl.BlockSpec(memory_space=pltpu.VMEM)
SMEM = pl.BlockSpec(memory_space=pltpu.SMEM)
HBM = pl.BlockSpec(memory_space=pltpu.HBM)
PARAMS = pltpu.CompilerParams(vmem_limit_bytes=40 * 1024 * 1024)
AXES = ("z_lo", "x", "core", "z_hi", "y_pair", "y_odd")
ROW = ("z_lo", "x", "core")
COL = ("z_hi", "y_pair", "y_odd")
QUAD = ("core", "y_odd")
HOME = ("core", "z_hi", "y_pair", "y_odd")
NEAR = ("x", "core")
Y = ("y_pair", "y_odd")
Z = ("z_lo", "z_hi")
SIZES = (4, 4, 2, 2, 4, 2)
SIDE = 16
PAIR = 8


def lanes_of(part):
    return slice(part * LANES, (part + 1) * LANES)


def quarter_kernel(features_ref, side_ref, out_ref):
    nodes = features_ref.shape[0]
    for part in range(out_ref.shape[0]):
        out_ref[part, :nodes, :] = features_ref[:, lanes_of(part)]
        out_ref[part, nodes:, :] = side_ref[...]


def tile_kernel(place_ref, meta_ref, *refs):
    given, block_ref, out_ref, tiles, total, sems = refs[:4], refs[4], refs[5], refs[6], refs[7], refs[8]
    _, slots, size, _ = tiles.shape
    n_x = block_ref.shape[0]
    core, odd = place_ref[0], place_ref[1]

    def tile_copy(which, slot):
        return pltpu.make_async_copy(
            given[which].at[slot], tiles.at[which, slot], sems.at[which, slot]
        )

    def cell_of(which):
        cell_core, cell_odd = (core + which // 2) % 2, (odd + which % 2) % 2
        return cell_core, cell_odd, cell_core * 2 + cell_odd

    for which in range(4):

        def fetch(slot, carry):
            tile_copy(which, slot).start()
            return carry

        lax.fori_loop(0, meta_ref[cell_of(which)[2], 2, 0], fetch, 0)
    total[...] = jnp.zeros_like(total)
    for which in range(4):
        cell_core, cell_odd, cell = cell_of(which)

        used = meta_ref[cell, 2, 0]

        def product(slot):
            chip = meta_ref[cell, 1, slot]
            z, x = chip // n_x, lax.rem(chip, n_x)
            window = jnp.concatenate(
                [block_ref[x, z, cell_odd], block_ref[x, z, 2 + cell_odd]], axis=0
            )
            return jnp.dot(tiles[which, slot], window, preferred_element_type=F32)

        def step(index, carry):
            slot = 2 * index
            both = slot + 1 < used
            other = jnp.where(both, slot + 1, slot)
            tile_copy(which, slot).wait()

            @pl.when(both)
            def _():
                tile_copy(which, other).wait()

            one, two = product(slot), product(other)
            total[cell_core, meta_ref[cell, 0, slot]] += one
            total[cell_core, meta_ref[cell, 0, other]] += jnp.where(both, two, 0.0)
            return carry

        lax.fori_loop(0, (used + 1) // 2, step, 0)
    out_ref[...] = total[...].astype(BF16)


def add(ref):
    total = ref[0].astype(F32)
    for part in range(1, ref.shape[0]):
        total = total + ref[part].astype(F32)
    return total


def repeat_kernel(given_ref, out_ref):
    for copy in range(out_ref.shape[0]):
        out_ref[copy] = given_ref[...]


def with_bias(main, row):
    high = row.astype(BF16).astype(F32)
    tall = (PAIR, row.shape[1])
    place = lax.broadcasted_iota(jnp.int32, tall, 0)
    high, low = (jnp.broadcast_to(part, tall) for part in (high, row - high))
    side = jnp.where(place == 0, high, jnp.where(place == 1, low, 0.0))
    return jnp.concatenate([main, side], axis=0).astype(BF16)


def bias_of(total):
    depth = total.shape[0] - PAIR
    return total[depth : depth + 1] + total[depth + 1 : depth + 2]


def node_kernel(parts_ref, weight_ref, bias_ref, cot_ref, act_ref, grads_ref):
    n_high, n_odd = parts_ref.shape[1], parts_ref.shape[2]
    quarters = []
    for core in range(parts_ref.shape[0]):
        for odd in range(n_odd):
            total = parts_ref[core, 0, odd].astype(F32)
            for high in range(1, n_high):
                total = total + parts_ref[core, high, odd].astype(F32)
            quarters.append(total.astype(BF16))
    aggregated = jnp.concatenate(quarters, axis=1)
    preact = jnp.dot(aggregated, weight_ref[...], preferred_element_type=F32) + bias_ref[...]
    sigmoid_part = jax.nn.sigmoid(preact)
    act_ref[...] = (preact * sigmoid_part).astype(BF16)
    grad = cot_ref[...].astype(F32) * sigmoid_part * (1.0 + preact * (1.0 - sigmoid_part))
    product = lax.dot_general(
        aggregated, grad.astype(BF16), (((0,), (0,)), ((), ())), preferred_element_type=F32
    )
    row = jnp.sum(grad, axis=0, keepdims=True)
    depth = grads_ref.shape[1] - PAIR
    for chunk in range(grads_ref.shape[0]):
        grads_ref[chunk] = with_bias(product[chunk * depth : (chunk + 1) * depth], row)


def scatter_kernel(parts_ref, out_ref):
    total = add(parts_ref)
    depth = out_ref.shape[1] - PAIR
    for chunk in range(out_ref.shape[0]):
        out_ref[chunk] = with_bias(total[chunk * depth : (chunk + 1) * depth], bias_of(total))


def sum_kernel(parts_ref, out_ref):
    total = add(parts_ref)
    rounded = with_bias(total[: total.shape[0] - PAIR], bias_of(total))
    for copy in range(out_ref.shape[0]):
        out_ref[copy] = rounded


def copy_kernel(parts_ref, out_ref):
    depth = parts_ref.shape[1] - PAIR
    parts = [parts_ref[part].astype(F32) for part in range(parts_ref.shape[0])]
    rows = jnp.concatenate([part[:depth] for part in parts] + [parts[0][depth:]], axis=0).astype(BF16)
    for copy in range(out_ref.shape[0]):
        out_ref[copy] = rows


def last_kernel(parts_ref, weight_ref, bias_ref):
    depth = parts_ref.shape[1] - PAIR
    for chunk in range(parts_ref.shape[0]):
        rows = parts_ref[chunk].astype(F32)
        weight_ref[chunk * depth : (chunk + 1) * depth] = rows[:depth]
        if chunk == 0:
            bias_ref[...] = bias_of(rows)


def call(kernel, out, *args, scalars=0):
    shapes = jax.tree.map(lambda o: jax.ShapeDtypeStruct(*o), out, is_leaf=lambda o: isinstance(o[0], tuple) and not isinstance(o[1], tuple))
    specs = jax.tree.map(lambda o: VMEM, shapes)
    return pl.pallas_call(
        kernel, out_shape=shapes, in_specs=[SMEM] * scalars + [VMEM] * (len(args) - scalars), out_specs=specs, compiler_params=PARAMS
    )(*args)


def swap(array, axis):
    return lax.ppermute(array, axis, [(0, 1), (1, 0)])


def per_device(
    features, weight, bias_term, cotangent, tile_values, tile_rows, tile_cols, tile_count
):
    nodes, width = features.shape
    _, _, slots, size, _ = tile_values.shape
    n_z, n_x = lax.axis_size("z_lo"), lax.axis_size("x")
    n_pair = lax.axis_size("y_pair")
    tiles = tile_values[0, 0]
    ints = [tile_rows[0, 0], tile_cols[0, 0], jnp.broadcast_to(tile_count[0], (slots,))]
    side = jnp.pad(jnp.stack(ints), ((0, SIDE - 3), (0, LANES - slots))).astype(BF16)
    quarters = call(quarter_kernel, ((4, nodes + SIDE, LANES), BF16), features, side)
    quarters = lax.all_to_all(quarters, QUAD, 0, 0)
    quarters, tiles = lax.optimization_barrier((quarters, tiles))
    tiles_y = swap(tiles, "y_odd")
    tiles_core = swap(tiles, "core")
    tiles_both = swap(tiles_y, "core")
    meta = quarters[:, nodes : nodes + 3, :slots].astype(jnp.int32)
    near = lax.all_gather(quarters[:, :nodes], "z_lo", axis=0)
    near = call(repeat_kernel, ((n_x,) + near.shape, BF16), near)
    blocks = lax.all_to_all(near, "x", 0, 0)
    place = jnp.stack([lax.axis_index(axis) for axis in QUAD]).astype(jnp.int32)
    term = pl.pallas_call(
        tile_kernel,
        out_shape=jax.ShapeDtypeStruct((2, 2 * n_pair, size, LANES), BF16),
        in_specs=[SMEM, SMEM] + [HBM] * 4 + [VMEM],
        out_specs=VMEM,
        scratch_shapes=[
            pltpu.VMEM((4, slots, size, size), BF16),
            pltpu.VMEM((2, 2 * n_pair, size, LANES), F32),
            pltpu.SemaphoreType.DMA((4, slots)),
        ],
        compiler_params=PARAMS,
    )(place, meta, tiles, tiles_y, tiles_core, tiles_both, blocks)
    shares = lax.all_to_all(term.reshape(-1, nodes, LANES), HOME, 0, 0)
    n_near, n_y, n_deep = lax.axis_size(NEAR), lax.axis_size(Y), lax.axis_size(Z)
    depth = width // n_near
    tall, short = depth + PAIR, depth // n_y + PAIR
    activations, grads = call(
        node_kernel,
        (((nodes, width), BF16), ((n_near, tall, width), BF16)),
        shares.reshape(2, 2 * n_pair, 2, nodes, LANES),
        weight,
        bias_term[None, :],
        cotangent,
    )
    grads = lax.all_to_all(grads, NEAR, 0, 0)
    grads = call(scatter_kernel, ((n_y, short, width), BF16), grads)
    grads = lax.all_to_all(grads, Y, 0, 0)
    grads = call(sum_kernel, ((n_deep, short, width), BF16), grads)
    grads = lax.all_to_all(grads, Z, 0, 0)
    grads = call(sum_kernel, ((n_y, short, width), BF16), grads)
    grads = lax.all_to_all(grads, Y, 0, 0)
    grads = call(copy_kernel, ((n_near, tall, width), BF16), grads)
    grads = lax.all_to_all(grads, NEAR, 0, 0)
    weight_grad, bias_grad = call(
        last_kernel, (((width, width), F32), ((1, width), F32)), grads
    )
    return activations, weight_grad, bias_grad[0]


def solution(mesh):
    cut = Mesh(mesh.devices.reshape(SIZES), AXES)
    everywhere = P(AXES, None)
    return jax.shard_map(
        per_device,
        mesh=cut,
        in_specs=(
            everywhere,
            P(),
            P(),
            everywhere,
            P(ROW, COL, None, None, None),
            P(ROW, COL, None),
            P(ROW, COL, None),
            P(ROW, COL),
        ),
        out_specs=(everywhere, P(), P()),
        check_vma=False,
    )
```

```python
import jax
import jax.numpy as jnp
from jax import lax
from jax.experimental import pallas as pl
from jax.experimental.pallas import tpu as pltpu
from jax.sharding import Mesh, PartitionSpec as P

F32 = jnp.float32
BF16 = jnp.bfloat16
LANES = 128
VMEM = pl.BlockSpec(memory_space=pltpu.VMEM)
SMEM = pl.BlockSpec(memory_space=pltpu.SMEM)
HBM = pl.BlockSpec(memory_space=pltpu.HBM)
PARAMS = pltpu.CompilerParams(vmem_limit_bytes=40 * 1024 * 1024)
AXES = ("z_lo", "x", "core", "z_hi", "y_pair", "y_odd")
ROW = ("z_lo", "x", "core")
COL = ("z_hi", "y_pair", "y_odd")
QUAD = ("core", "y_odd")
HOME = ("core", "y_pair", "y_odd", "z_hi")
NEAR = ("x", "core")
Y = ("y_pair", "y_odd")
Z = ("z_lo", "z_hi")
SIZES = (4, 4, 2, 2, 4, 2)
SIDE = 16
PAIR = 8


def lanes_of(part):
    return slice(part * LANES, (part + 1) * LANES)


def quarter_kernel(features_ref, side_ref, out_ref):
    nodes = features_ref.shape[0]
    for part in range(out_ref.shape[0]):
        out_ref[part, :nodes, :] = features_ref[:, lanes_of(part)]
        out_ref[part, nodes:, :] = side_ref[...]


def tile_kernel(place_ref, meta_ref, *refs):
    given, block_ref, out_ref, tiles, total, sems = refs[:4], refs[4], refs[5], refs[6], refs[7], refs[8]
    _, slots, size, _ = tiles.shape
    n_x = block_ref.shape[0]
    core, odd = place_ref[0], place_ref[1]

    def tile_copy(which, slot):
        return pltpu.make_async_copy(
            given[which].at[slot], tiles.at[which, slot], sems.at[which, slot]
        )

    def cell_of(which):
        cell_core, cell_odd = (core + which // 2) % 2, (odd + which % 2) % 2
        return cell_core, cell_odd, cell_core * 2 + cell_odd

    for which in range(4):

        def fetch(slot, carry):
            tile_copy(which, slot).start()
            return carry

        lax.fori_loop(0, meta_ref[cell_of(which)[2], 2, 0], fetch, 0)
    total[...] = jnp.zeros_like(total)
    for which in range(4):
        cell_core, cell_odd, cell = cell_of(which)

        used = meta_ref[cell, 2, 0]

        def product(slot):
            chip = meta_ref[cell, 1, slot]
            z, x = chip // n_x, lax.rem(chip, n_x)
            window = jnp.concatenate(
                [block_ref[x, z, cell_odd], block_ref[x, z, 2 + cell_odd]], axis=0
            )
            return jnp.dot(tiles[which, slot], window, preferred_element_type=F32)

        def step(index, carry):
            slot = 2 * index
            both = slot + 1 < used
            other = jnp.where(both, slot + 1, slot)
            tile_copy(which, slot).wait()

            @pl.when(both)
            def _():
                tile_copy(which, other).wait()

            one, two = product(slot), product(other)
            total[cell_core, meta_ref[cell, 0, slot]] += one
            total[cell_core, meta_ref[cell, 0, other]] += jnp.where(both, two, 0.0)
            return carry

        lax.fori_loop(0, (used + 1) // 2, step, 0)
    n_pair, nodes = out_ref.shape[1], out_ref.shape[4]
    for cell_core in range(2):
        for pair in range(n_pair):
            for high in range(2):
                rows = total[cell_core, high * n_pair + pair].astype(BF16)
                for cell_odd in range(2):
                    out_ref[cell_core, pair, cell_odd, high] = rows[
                        cell_odd * nodes : (cell_odd + 1) * nodes
                    ]


def add(ref):
    total = ref[0].astype(F32)
    for part in range(1, ref.shape[0]):
        total = total + ref[part].astype(F32)
    return total


def repeat_kernel(given_ref, out_ref):
    for copy in range(out_ref.shape[0]):
        out_ref[copy] = given_ref[...]


def with_bias(main, row):
    high = row.astype(BF16).astype(F32)
    tall = (PAIR, row.shape[1])
    place = lax.broadcasted_iota(jnp.int32, tall, 0)
    high, low = (jnp.broadcast_to(part, tall) for part in (high, row - high))
    side = jnp.where(place == 0, high, jnp.where(place == 1, low, 0.0))
    return jnp.concatenate([main, side], axis=0).astype(BF16)


def bias_of(total):
    depth = total.shape[0] - PAIR
    return total[depth : depth + 1] + total[depth + 1 : depth + 2]


def node_kernel(parts_ref, weight_ref, bias_ref, cot_ref, act_ref, grads_ref):
    n_core, n_pair, n_odd, n_high = parts_ref.shape[:4]
    quarters = []
    for core in range(n_core):
        for odd in range(n_odd):
            senders = [(pair, high) for pair in range(n_pair) for high in range(n_high)]
            total = parts_ref[core, 0, odd, 0].astype(F32)
            for pair, high in senders[1:]:
                total = total + parts_ref[core, pair, odd, high].astype(F32)
            quarters.append(total.astype(BF16))
    aggregated = jnp.concatenate(quarters, axis=1)
    preact = jnp.dot(aggregated, weight_ref[...], preferred_element_type=F32) + bias_ref[...]
    sigmoid_part = jax.nn.sigmoid(preact)
    act_ref[...] = (preact * sigmoid_part).astype(BF16)
    grad = cot_ref[...].astype(F32) * sigmoid_part * (1.0 + preact * (1.0 - sigmoid_part))
    product = lax.dot_general(
        aggregated, grad.astype(BF16), (((0,), (0,)), ((), ())), preferred_element_type=F32
    )
    row = jnp.sum(grad, axis=0, keepdims=True)
    depth = grads_ref.shape[1] - PAIR
    for chunk in range(grads_ref.shape[0]):
        grads_ref[chunk] = with_bias(product[chunk * depth : (chunk + 1) * depth], row)


def scatter_kernel(parts_ref, out_ref):
    total = add(parts_ref)
    depth = out_ref.shape[1] - PAIR
    for chunk in range(out_ref.shape[0]):
        out_ref[chunk] = with_bias(total[chunk * depth : (chunk + 1) * depth], bias_of(total))


def sum_kernel(parts_ref, out_ref):
    total = add(parts_ref)
    rounded = with_bias(total[: total.shape[0] - PAIR], bias_of(total))
    for copy in range(out_ref.shape[0]):
        out_ref[copy] = rounded


def copy_kernel(parts_ref, out_ref):
    depth = parts_ref.shape[1] - PAIR
    parts = [parts_ref[part].astype(F32) for part in range(parts_ref.shape[0])]
    rows = jnp.concatenate([part[:depth] for part in parts] + [parts[0][depth:]], axis=0).astype(BF16)
    for copy in range(out_ref.shape[0]):
        out_ref[copy] = rows


def last_kernel(place_ref, own_ref, other_ref, weight_ref, bias_ref):
    depth = own_ref.shape[1] - PAIR
    for chunk in range(own_ref.shape[0]):
        for core, ref in ((place_ref[0], own_ref), (1 - place_ref[0], other_ref)):
            rows = pl.ds(pl.multiple_of((chunk * 2 + core) * depth, depth), depth)
            part = ref[chunk].astype(F32)
            weight_ref[rows] = part[:depth]
    bias_ref[...] = bias_of(own_ref[0].astype(F32))


def call(kernel, out, *args, scalars=0):
    shapes = jax.tree.map(lambda o: jax.ShapeDtypeStruct(*o), out, is_leaf=lambda o: isinstance(o[0], tuple) and not isinstance(o[1], tuple))
    specs = jax.tree.map(lambda o: VMEM, shapes)
    return pl.pallas_call(
        kernel, out_shape=shapes, in_specs=[SMEM] * scalars + [VMEM] * (len(args) - scalars), out_specs=specs, compiler_params=PARAMS
    )(*args)


def swap(array, axis):
    return lax.ppermute(array, axis, [(0, 1), (1, 0)])


def per_device(
    features, weight, bias_term, cotangent, tile_values, tile_rows, tile_cols, tile_count
):
    nodes, width = features.shape
    _, _, slots, size, _ = tile_values.shape
    n_z, n_x = lax.axis_size("z_lo"), lax.axis_size("x")
    n_pair = lax.axis_size("y_pair")
    tiles = tile_values[0, 0]
    ints = [tile_rows[0, 0], tile_cols[0, 0], jnp.broadcast_to(tile_count[0], (slots,))]
    side = jnp.pad(jnp.stack(ints), ((0, SIDE - 3), (0, LANES - slots))).astype(BF16)
    quarters = call(quarter_kernel, ((4, nodes + SIDE, LANES), BF16), features, side)
    quarters = lax.all_to_all(quarters, QUAD, 0, 0)
    quarters, tiles = lax.optimization_barrier((quarters, tiles))
    tiles_y = swap(tiles, "y_odd")
    tiles_core = swap(tiles, "core")
    tiles_both = swap(tiles_y, "core")
    meta = quarters[:, nodes : nodes + 3, :slots].astype(jnp.int32)
    near = lax.all_gather(quarters[:, :nodes], "z_lo", axis=0)
    near = call(repeat_kernel, ((n_x,) + near.shape, BF16), near)
    blocks = lax.all_to_all(near, "x", 0, 0)
    place = jnp.stack([lax.axis_index(axis) for axis in QUAD]).astype(jnp.int32)
    term = pl.pallas_call(
        tile_kernel,
        out_shape=jax.ShapeDtypeStruct((2, n_pair, 2, 2, nodes, LANES), BF16),
        in_specs=[SMEM, SMEM] + [HBM] * 4 + [VMEM],
        out_specs=VMEM,
        scratch_shapes=[
            pltpu.VMEM((4, slots, size, size), BF16),
            pltpu.VMEM((2, 2 * n_pair, size, LANES), F32),
            pltpu.SemaphoreType.DMA((4, slots)),
        ],
        compiler_params=PARAMS,
    )(place, meta, tiles, tiles_y, tiles_core, tiles_both, blocks)
    shares = lax.all_to_all(term.reshape(-1, nodes, LANES), HOME, 0, 0)
    n_near, n_y, n_deep = lax.axis_size(NEAR), lax.axis_size(Y), lax.axis_size(Z)
    depth = width // n_near
    tall, short = depth + PAIR, depth // n_y + PAIR
    activations, grads = call(
        node_kernel,
        (((nodes, width), BF16), ((n_near, tall, width), BF16)),
        shares.reshape(2, n_pair, 2, 2, nodes, LANES),
        weight,
        bias_term[None, :],
        cotangent,
    )
    grads = lax.all_to_all(grads, NEAR, 0, 0)
    grads = call(scatter_kernel, ((n_y, short, width), BF16), grads)
    grads = lax.all_to_all(grads, Y, 0, 0)
    grads = call(sum_kernel, ((n_deep, short, width), BF16), grads)
    grads = lax.all_to_all(grads, Z, 0, 0)
    grads = call(sum_kernel, ((n_y, short, width), BF16), grads)
    grads = lax.all_to_all(grads, Y, 0, 0)
    grads = call(copy_kernel, ((n_x, tall, width), BF16), grads)
    grads = lax.all_to_all(grads, "x", 0, 0)
    weight_grad, bias_grad = call(
        last_kernel,
        (((width, width), F32), ((1, width), F32)),
        place,
        grads,
        swap(grads, "core"),
        scalars=1,
    )
    return activations, weight_grad, bias_grad[0]


def solution(mesh):
    cut = Mesh(mesh.devices.reshape(SIZES), AXES)
    everywhere = P(AXES, None)
    return jax.shard_map(
        per_device,
        mesh=cut,
        in_specs=(
            everywhere,
            P(),
            P(),
            everywhere,
            P(ROW, COL, None, None, None),
            P(ROW, COL, None),
            P(ROW, COL, None),
            P(ROW, COL),
        ),
        out_specs=(everywhere, P(), P()),
        check_vma=False,
    )
```

```python
import jax
import jax.numpy as jnp
from jax import lax
from jax.experimental import pallas as pl
from jax.experimental.pallas import tpu as pltpu
from jax.sharding import Mesh, PartitionSpec as P

F32 = jnp.float32
BF16 = jnp.bfloat16
LANES = 128
VMEM = pl.BlockSpec(memory_space=pltpu.VMEM)
SMEM = pl.BlockSpec(memory_space=pltpu.SMEM)
HBM = pl.BlockSpec(memory_space=pltpu.HBM)
PARAMS = pltpu.CompilerParams(vmem_limit_bytes=40 * 1024 * 1024)
AXES = ("z_lo", "x", "core", "z_hi", "y_pair", "y_odd")
ROW = ("z_lo", "x", "core")
COL = ("z_hi", "y_pair", "y_odd")
QUAD = ("core", "y_odd")
HOME = ("core", "y_pair", "y_odd", "z_hi")
NEAR = ("x", "core")
Y = ("y_pair", "y_odd")
Z = ("z_lo", "z_hi")
SIZES = (4, 4, 2, 2, 4, 2)
SIDE = 16
PAIR = 8


def lanes_of(part):
    return slice(part * LANES, (part + 1) * LANES)


def quarter_kernel(features_ref, side_ref, out_ref):
    nodes = features_ref.shape[0]
    for part in range(out_ref.shape[0]):
        out_ref[part, :nodes, :] = features_ref[:, lanes_of(part)]
        out_ref[part, nodes:, :] = side_ref[...]


def tile_kernel(place_ref, meta_ref, *refs):
    given, block_ref, out_ref, total = refs[:4], refs[4], refs[5], refs[6]
    n_x = block_ref.shape[0]
    core, odd = place_ref[0], place_ref[1]

    def cell_of(which):
        cell_core, cell_odd = (core + which // 2) % 2, (odd + which % 2) % 2
        return cell_core, cell_odd, cell_core * 2 + cell_odd

    total[...] = jnp.zeros_like(total)
    for which in range(4):
        cell_core, cell_odd, cell = cell_of(which)

        used = meta_ref[cell, 2, 0]

        def product(slot):
            chip = meta_ref[cell, 1, slot]
            z, x = chip // n_x, lax.rem(chip, n_x)
            window = jnp.concatenate(
                [block_ref[x, z, cell_odd], block_ref[x, z, 2 + cell_odd]], axis=0
            )
            return jnp.dot(given[which][slot], window, preferred_element_type=F32)

        def step(index, carry):
            slot = 2 * index
            both = slot + 1 < used
            other = jnp.where(both, slot + 1, slot)
            one, two = product(slot), product(other)
            total[cell_core, meta_ref[cell, 0, slot]] += one
            total[cell_core, meta_ref[cell, 0, other]] += jnp.where(both, two, 0.0)
            return carry

        lax.fori_loop(0, (used + 1) // 2, step, 0)
    n_pair, nodes = out_ref.shape[1], out_ref.shape[4]
    for cell_core in range(2):
        for pair in range(n_pair):
            for high in range(2):
                rows = total[cell_core, high * n_pair + pair].astype(BF16)
                for cell_odd in range(2):
                    out_ref[cell_core, pair, cell_odd, high] = rows[
                        cell_odd * nodes : (cell_odd + 1) * nodes
                    ]


def add(ref):
    total = ref[0].astype(F32)
    for part in range(1, ref.shape[0]):
        total = total + ref[part].astype(F32)
    return total


def repeat_kernel(given_ref, out_ref, sems):
    copies = [
        pltpu.make_async_copy(given_ref, out_ref.at[copy], sems.at[copy])
        for copy in range(out_ref.shape[0])
    ]
    for copy in copies:
        copy.start()
    for copy in copies:
        copy.wait()


def with_bias(main, row):
    high = row.astype(BF16).astype(F32)
    tall = (PAIR, row.shape[1])
    place = lax.broadcasted_iota(jnp.int32, tall, 0)
    high, low = (jnp.broadcast_to(part, tall) for part in (high, row - high))
    side = jnp.where(place == 0, high, jnp.where(place == 1, low, 0.0))
    return jnp.concatenate([main, side], axis=0).astype(BF16)


def bias_of(total):
    depth = total.shape[0] - PAIR
    return total[depth : depth + 1] + total[depth + 1 : depth + 2]


def node_kernel(parts_ref, weight_ref, bias_ref, cot_ref, act_ref, grads_ref):
    n_core, n_pair, n_odd, n_high = parts_ref.shape[:4]
    quarters = []
    for core in range(n_core):
        for odd in range(n_odd):
            senders = [(pair, high) for pair in range(n_pair) for high in range(n_high)]
            total = parts_ref[core, 0, odd, 0].astype(F32)
            for pair, high in senders[1:]:
                total = total + parts_ref[core, pair, odd, high].astype(F32)
            quarters.append(total.astype(BF16))
    aggregated = jnp.concatenate(quarters, axis=1)
    preact = jnp.dot(aggregated, weight_ref[...], preferred_element_type=F32) + bias_ref[...]
    sigmoid_part = jax.nn.sigmoid(preact)
    act_ref[...] = (preact * sigmoid_part).astype(BF16)
    grad = cot_ref[...].astype(F32) * sigmoid_part * (1.0 + preact * (1.0 - sigmoid_part))
    product = lax.dot_general(
        aggregated, grad.astype(BF16), (((0,), (0,)), ((), ())), preferred_element_type=F32
    )
    row = jnp.sum(grad, axis=0, keepdims=True)
    depth = grads_ref.shape[1] - PAIR
    for chunk in range(grads_ref.shape[0]):
        grads_ref[chunk] = with_bias(product[chunk * depth : (chunk + 1) * depth], row)


def scatter_kernel(parts_ref, out_ref):
    total = add(parts_ref)
    depth = out_ref.shape[1] - PAIR
    for chunk in range(out_ref.shape[0]):
        out_ref[chunk] = with_bias(total[chunk * depth : (chunk + 1) * depth], bias_of(total))


def sum_kernel(parts_ref, out_ref):
    total = add(parts_ref)
    rounded = with_bias(total[: total.shape[0] - PAIR], bias_of(total))
    for copy in range(out_ref.shape[0]):
        out_ref[copy] = rounded


def copy_kernel(parts_ref, out_ref):
    depth = parts_ref.shape[1] - PAIR
    parts = [parts_ref[part].astype(F32) for part in range(parts_ref.shape[0])]
    rows = jnp.concatenate([part[:depth] for part in parts] + [parts[0][depth:]], axis=0).astype(BF16)
    for copy in range(out_ref.shape[0]):
        out_ref[copy] = rows


def last_kernel(parts_ref, weight_ref, bias_ref):
    depth = parts_ref.shape[1] - PAIR
    for chunk in range(parts_ref.shape[0]):
        rows = parts_ref[chunk].astype(F32)
        weight_ref[chunk * depth : (chunk + 1) * depth] = rows[:depth]
        if chunk == 0:
            bias_ref[...] = bias_of(rows)


def call(kernel, out, *args, scalars=0):
    shapes = jax.tree.map(lambda o: jax.ShapeDtypeStruct(*o), out, is_leaf=lambda o: isinstance(o[0], tuple) and not isinstance(o[1], tuple))
    specs = jax.tree.map(lambda o: VMEM, shapes)
    return pl.pallas_call(
        kernel, out_shape=shapes, in_specs=[SMEM] * scalars + [VMEM] * (len(args) - scalars), out_specs=specs, compiler_params=PARAMS
    )(*args)


def swap(array, axis):
    return lax.ppermute(array, axis, [(0, 1), (1, 0)])


def per_device(
    features, weight, bias_term, cotangent, tile_values, tile_rows, tile_cols, tile_count
):
    nodes, width = features.shape
    _, _, slots, size, _ = tile_values.shape
    n_z, n_x = lax.axis_size("z_lo"), lax.axis_size("x")
    n_pair = lax.axis_size("y_pair")
    tiles = tile_values[0, 0]
    ints = [tile_rows[0, 0], tile_cols[0, 0], jnp.broadcast_to(tile_count[0], (slots,))]
    side = jnp.pad(jnp.stack(ints), ((0, SIDE - 3), (0, LANES - slots))).astype(BF16)
    quarters = call(quarter_kernel, ((4, nodes + SIDE, LANES), BF16), features, side)
    quarters = lax.all_to_all(quarters, QUAD, 0, 0)
    quarters, tiles = lax.optimization_barrier((quarters, tiles))
    tiles_y = swap(tiles, "y_odd")
    tiles_core = swap(tiles, "core")
    tiles_both = swap(tiles_y, "core")
    meta = quarters[:, nodes : nodes + 3, :slots].astype(jnp.int32)
    near = lax.all_gather(quarters[:, :nodes], "z_lo", axis=0)
    near = pl.pallas_call(
        repeat_kernel,
        out_shape=jax.ShapeDtypeStruct((n_x,) + near.shape, BF16),
        in_specs=[VMEM],
        out_specs=HBM,
        scratch_shapes=[pltpu.SemaphoreType.DMA((n_x,))],
        compiler_params=PARAMS,
    )(near)
    blocks = lax.all_to_all(near, "x", 0, 0)
    place = jnp.stack([lax.axis_index(axis) for axis in QUAD]).astype(jnp.int32)
    term = pl.pallas_call(
        tile_kernel,
        out_shape=jax.ShapeDtypeStruct((2, n_pair, 2, 2, nodes, LANES), BF16),
        in_specs=[SMEM, SMEM] + [VMEM] * 5,
        out_specs=VMEM,
        scratch_shapes=[
            pltpu.VMEM((2, 2 * n_pair, size, LANES), F32),
        ],
        compiler_params=PARAMS,
    )(place, meta, tiles, tiles_y, tiles_core, tiles_both, blocks)
    shares = lax.all_to_all(term.reshape(-1, nodes, LANES), HOME, 0, 0)
    n_near, n_y, n_deep = lax.axis_size(NEAR), lax.axis_size(Y), lax.axis_size(Z)
    depth = width // n_near
    tall, short = depth + PAIR, depth // n_y + PAIR
    activations, grads = call(
        node_kernel,
        (((nodes, width), BF16), ((n_near, tall, width), BF16)),
        shares.reshape(2, n_pair, 2, 2, nodes, LANES),
        weight,
        bias_term[None, :],
        cotangent,
    )
    grads = lax.all_to_all(grads, NEAR, 0, 0)
    grads = call(scatter_kernel, ((n_y, short, width), BF16), grads)
    grads = lax.all_to_all(grads, Y, 0, 0)
    grads = call(sum_kernel, ((n_deep, short, width), BF16), grads)
    grads = lax.all_to_all(grads, Z, 0, 0)
    grads = call(sum_kernel, ((n_y, short, width), BF16), grads)
    grads = lax.all_to_all(grads, Y, 0, 0)
    grads = call(copy_kernel, ((n_near, tall, width), BF16), grads)
    grads = lax.all_to_all(grads, NEAR, 0, 0)
    weight_grad, bias_grad = call(
        last_kernel, (((width, width), F32), ((1, width), F32)), grads
    )
    return activations, weight_grad, bias_grad[0]


def solution(mesh):
    cut = Mesh(mesh.devices.reshape(SIZES), AXES)
    everywhere = P(AXES, None)
    return jax.shard_map(
        per_device,
        mesh=cut,
        in_specs=(
            everywhere,
            P(),
            P(),
            everywhere,
            P(ROW, COL, None, None, None),
            P(ROW, COL, None),
            P(ROW, COL, None),
            P(ROW, COL),
        ),
        out_specs=(everywhere, P(), P()),
        check_vma=False,
    )
```

```python
import jax
import jax.numpy as jnp
from jax import lax
from jax.experimental import pallas as pl
from jax.experimental.pallas import tpu as pltpu
from jax.sharding import Mesh, PartitionSpec as P

F32 = jnp.float32
BF16 = jnp.bfloat16
LANES = 128
VMEM = pl.BlockSpec(memory_space=pltpu.VMEM)
SMEM = pl.BlockSpec(memory_space=pltpu.SMEM)
HBM = pl.BlockSpec(memory_space=pltpu.HBM)
PARAMS = pltpu.CompilerParams(vmem_limit_bytes=40 * 1024 * 1024)
AXES = ("z_lo", "x", "core", "z_hi", "y_pair", "y_odd")
ROW = ("z_lo", "x", "core")
COL = ("z_hi", "y_pair", "y_odd")
QUAD = ("core", "y_odd")
HOME = ("core", "y_pair", "y_odd", "z_hi")
NEAR = ("x", "core")
Y = ("y_pair", "y_odd")
Z = ("z_lo", "z_hi")
SIZES = (4, 4, 2, 2, 4, 2)
SIDE = 16
PAIR = 8


def lanes_of(part):
    return slice(part * LANES, (part + 1) * LANES)


def quarter_kernel(features_ref, side_ref, out_ref):
    nodes = features_ref.shape[0]
    for part in range(out_ref.shape[0]):
        out_ref[part, :nodes, :] = features_ref[:, lanes_of(part)]
        out_ref[part, nodes:, :] = side_ref[...]


def tile_kernel(place_ref, meta_ref, *refs):
    given, block_ref, out_ref, total = refs[:4], refs[4], refs[5], refs[6]
    n_x = block_ref.shape[0]
    core, odd = place_ref[0], place_ref[1]

    def cell_of(which):
        cell_core, cell_odd = (core + which // 2) % 2, (odd + which % 2) % 2
        return cell_core, cell_odd, cell_core * 2 + cell_odd

    total[...] = jnp.zeros_like(total)
    for which in range(4):
        cell_core, cell_odd, cell = cell_of(which)

        used = meta_ref[cell, 2, 0]

        def product(slot):
            chip = meta_ref[cell, 1, slot]
            z, x = chip // n_x, lax.rem(chip, n_x)
            window = jnp.concatenate(
                [block_ref[x, z, cell_odd], block_ref[x, z, 2 + cell_odd]], axis=0
            )
            return jnp.dot(given[which][slot], window, preferred_element_type=F32)

        def step(index, carry):
            slot = 2 * index
            both = slot + 1 < used
            other = jnp.where(both, slot + 1, slot)
            one, two = product(slot), product(other)
            total[cell_core, meta_ref[cell, 0, slot]] += one
            total[cell_core, meta_ref[cell, 0, other]] += jnp.where(both, two, 0.0)
            return carry

        lax.fori_loop(0, (used + 1) // 2, step, 0)
    n_pair, nodes = out_ref.shape[1], out_ref.shape[4]
    for cell_core in range(2):
        for pair in range(n_pair):
            for high in range(2):
                rows = total[cell_core, high * n_pair + pair].astype(BF16)
                for cell_odd in range(2):
                    out_ref[cell_core, pair, cell_odd, high] = rows[
                        cell_odd * nodes : (cell_odd + 1) * nodes
                    ]


def add(ref):
    total = ref[0].astype(F32)
    for part in range(1, ref.shape[0]):
        total = total + ref[part].astype(F32)
    return total


def repeat_kernel(given_ref, out_ref, sems):
    given = given_ref.at[:, pl.ds(0, out_ref.shape[2])]
    copies = [
        pltpu.make_async_copy(given, out_ref.at[copy], sems.at[copy])
        for copy in range(out_ref.shape[0])
    ]
    for copy in copies:
        copy.start()
    for copy in copies:
        copy.wait()


def with_bias(main, row):
    high = row.astype(BF16).astype(F32)
    tall = (PAIR, row.shape[1])
    place = lax.broadcasted_iota(jnp.int32, tall, 0)
    high, low = (jnp.broadcast_to(part, tall) for part in (high, row - high))
    side = jnp.where(place == 0, high, jnp.where(place == 1, low, 0.0))
    return jnp.concatenate([main, side], axis=0).astype(BF16)


def bias_of(total):
    depth = total.shape[0] - PAIR
    return total[depth : depth + 1] + total[depth + 1 : depth + 2]


def node_kernel(parts_ref, weight_ref, bias_ref, cot_ref, act_ref, grads_ref):
    n_core, n_pair, n_odd, n_high = parts_ref.shape[:4]
    quarters = []
    for core in range(n_core):
        for odd in range(n_odd):
            senders = [(pair, high) for pair in range(n_pair) for high in range(n_high)]
            total = parts_ref[core, 0, odd, 0].astype(F32)
            for pair, high in senders[1:]:
                total = total + parts_ref[core, pair, odd, high].astype(F32)
            quarters.append(total.astype(BF16))
    aggregated = jnp.concatenate(quarters, axis=1)
    preact = jnp.dot(aggregated, weight_ref[...], preferred_element_type=F32) + bias_ref[...]
    sigmoid_part = jax.nn.sigmoid(preact)
    act_ref[...] = (preact * sigmoid_part).astype(BF16)
    grad = cot_ref[...].astype(F32) * sigmoid_part * (1.0 + preact * (1.0 - sigmoid_part))
    product = lax.dot_general(
        aggregated, grad.astype(BF16), (((0,), (0,)), ((), ())), preferred_element_type=F32
    )
    row = jnp.sum(grad, axis=0, keepdims=True)
    depth = grads_ref.shape[1] - PAIR
    for chunk in range(grads_ref.shape[0]):
        grads_ref[chunk] = with_bias(product[chunk * depth : (chunk + 1) * depth], row)


def scatter_kernel(parts_ref, out_ref):
    total = add(parts_ref)
    depth = out_ref.shape[1] - PAIR
    for chunk in range(out_ref.shape[0]):
        out_ref[chunk] = with_bias(total[chunk * depth : (chunk + 1) * depth], bias_of(total))


def sum_kernel(parts_ref, out_ref):
    total = add(parts_ref)
    rounded = with_bias(total[: total.shape[0] - PAIR], bias_of(total))
    for copy in range(out_ref.shape[0]):
        out_ref[copy] = rounded


def copy_kernel(parts_ref, out_ref):
    depth = parts_ref.shape[1] - PAIR
    parts = [parts_ref[part].astype(F32) for part in range(parts_ref.shape[0])]
    rows = jnp.concatenate([part[:depth] for part in parts] + [parts[0][depth:]], axis=0).astype(BF16)
    for copy in range(out_ref.shape[0]):
        out_ref[copy] = rows


def last_kernel(parts_ref, weight_ref, bias_ref):
    depth = parts_ref.shape[1] - PAIR
    for chunk in range(parts_ref.shape[0]):
        rows = parts_ref[chunk].astype(F32)
        weight_ref[chunk * depth : (chunk + 1) * depth] = rows[:depth]
        if chunk == 0:
            bias_ref[...] = bias_of(rows)


def call(kernel, out, *args, scalars=0):
    shapes = jax.tree.map(lambda o: jax.ShapeDtypeStruct(*o), out, is_leaf=lambda o: isinstance(o[0], tuple) and not isinstance(o[1], tuple))
    specs = jax.tree.map(lambda o: VMEM, shapes)
    return pl.pallas_call(
        kernel, out_shape=shapes, in_specs=[SMEM] * scalars + [VMEM] * (len(args) - scalars), out_specs=specs, compiler_params=PARAMS
    )(*args)


def repeat(array, copies, rows):
    return pl.pallas_call(
        repeat_kernel,
        out_shape=jax.ShapeDtypeStruct((copies, array.shape[0], rows, LANES), BF16),
        in_specs=[VMEM],
        out_specs=HBM,
        scratch_shapes=[pltpu.SemaphoreType.DMA((copies,))],
        compiler_params=PARAMS,
    )(array)


def swap(array, axis):
    return lax.ppermute(array, axis, [(0, 1), (1, 0)])


def per_device(
    features, weight, bias_term, cotangent, tile_values, tile_rows, tile_cols, tile_count
):
    nodes, width = features.shape
    _, _, slots, size, _ = tile_values.shape
    n_z, n_x = lax.axis_size("z_lo"), lax.axis_size("x")
    n_pair = lax.axis_size("y_pair")
    tiles = tile_values[0, 0]
    ints = [tile_rows[0, 0], tile_cols[0, 0], jnp.broadcast_to(tile_count[0], (slots,))]
    side = jnp.pad(jnp.stack(ints), ((0, SIDE - 3), (0, LANES - slots))).astype(BF16)
    quarters = call(quarter_kernel, ((4, nodes + SIDE, LANES), BF16), features, side)
    quarters = lax.all_to_all(quarters, QUAD, 0, 0)
    quarters, tiles = lax.optimization_barrier((quarters, tiles))
    tiles_y = swap(tiles, "y_odd")
    tiles_core = swap(tiles, "core")
    tiles_both = swap(tiles_y, "core")
    meta = quarters[:, nodes : nodes + 3, :slots].astype(jnp.int32)
    near = lax.all_to_all(repeat(quarters, n_z, nodes), "z_lo", 0, 0)
    near = repeat(near.reshape(-1, nodes, LANES), n_x, nodes).reshape((n_x,) + near.shape)
    blocks = lax.all_to_all(near, "x", 0, 0)
    place = jnp.stack([lax.axis_index(axis) for axis in QUAD]).astype(jnp.int32)
    term = pl.pallas_call(
        tile_kernel,
        out_shape=jax.ShapeDtypeStruct((2, n_pair, 2, 2, nodes, LANES), BF16),
        in_specs=[SMEM, SMEM] + [VMEM] * 5,
        out_specs=VMEM,
        scratch_shapes=[
            pltpu.VMEM((2, 2 * n_pair, size, LANES), F32),
        ],
        compiler_params=PARAMS,
    )(place, meta, tiles, tiles_y, tiles_core, tiles_both, blocks)
    shares = lax.all_to_all(term.reshape(-1, nodes, LANES), HOME, 0, 0)
    n_near, n_y, n_deep = lax.axis_size(NEAR), lax.axis_size(Y), lax.axis_size(Z)
    depth = width // n_near
    tall, short = depth + PAIR, depth // n_y + PAIR
    activations, grads = call(
        node_kernel,
        (((nodes, width), BF16), ((n_near, tall, width), BF16)),
        shares.reshape(2, n_pair, 2, 2, nodes, LANES),
        weight,
        bias_term[None, :],
        cotangent,
    )
    grads = lax.all_to_all(grads, NEAR, 0, 0)
    grads = call(scatter_kernel, ((n_y, short, width), BF16), grads)
    grads = lax.all_to_all(grads, Y, 0, 0)
    grads = call(sum_kernel, ((n_deep, short, width), BF16), grads)
    grads = lax.all_to_all(grads, Z, 0, 0)
    grads = call(sum_kernel, ((n_y, short, width), BF16), grads)
    grads = lax.all_to_all(grads, Y, 0, 0)
    grads = call(copy_kernel, ((n_near, tall, width), BF16), grads)
    grads = lax.all_to_all(grads, NEAR, 0, 0)
    weight_grad, bias_grad = call(
        last_kernel, (((width, width), F32), ((1, width), F32)), grads
    )
    return activations, weight_grad, bias_grad[0]


def solution(mesh):
    cut = Mesh(mesh.devices.reshape(SIZES), AXES)
    everywhere = P(AXES, None)
    return jax.shard_map(
        per_device,
        mesh=cut,
        in_specs=(
            everywhere,
            P(),
            P(),
            everywhere,
            P(ROW, COL, None, None, None),
            P(ROW, COL, None),
            P(ROW, COL, None),
            P(ROW, COL),
        ),
        out_specs=(everywhere, P(), P()),
        check_vma=False,
    )
```

```python
import jax
import jax.numpy as jnp
from jax import lax
from jax.experimental import pallas as pl
from jax.experimental.pallas import tpu as pltpu
from jax.sharding import Mesh, PartitionSpec as P

F32 = jnp.float32
BF16 = jnp.bfloat16
LANES = 128
VMEM = pl.BlockSpec(memory_space=pltpu.VMEM)
SMEM = pl.BlockSpec(memory_space=pltpu.SMEM)
HBM = pl.BlockSpec(memory_space=pltpu.HBM)
PARAMS = pltpu.CompilerParams(vmem_limit_bytes=40 * 1024 * 1024)
AXES = ("z_lo", "x", "core", "z_hi", "y_pair", "y_odd")
ROW = ("z_lo", "x", "core")
COL = ("z_hi", "y_pair", "y_odd")
QUAD = ("core", "y_odd")
HOME = ("core", "y_pair", "y_odd", "z_hi")
NEAR = ("x", "core")
Y = ("y_pair", "y_odd")
Z = ("z_lo", "z_hi")
SIZES = (4, 4, 2, 2, 4, 2)
SIDE = 16
PAIR = 8


def lanes_of(part):
    return slice(part * LANES, (part + 1) * LANES)


def quarter_kernel(features_ref, side_ref, out_ref):
    nodes = features_ref.shape[0]
    for part in range(out_ref.shape[0]):
        out_ref[part, :nodes, :] = features_ref[:, lanes_of(part)]
        out_ref[part, nodes:, :] = side_ref[...]


def tile_kernel(place_ref, meta_ref, *refs):
    given, block_ref, out_ref, total = refs[:4], refs[4], refs[5], refs[6]
    n_x = block_ref.shape[0]
    core, odd = place_ref[0], place_ref[1]

    def cell_of(which):
        cell_core, cell_odd = (core + which // 2) % 2, (odd + which % 2) % 2
        return cell_core, cell_odd, cell_core * 2 + cell_odd

    total[...] = jnp.zeros_like(total)
    for which in range(4):
        cell_core, cell_odd, cell = cell_of(which)

        used = meta_ref[cell, 2, 0]

        def product(slot):
            chip = meta_ref[cell, 1, slot]
            z, x = chip // n_x, lax.rem(chip, n_x)
            window = jnp.concatenate(
                [block_ref[x, z, cell_odd], block_ref[x, z, 2 + cell_odd]], axis=0
            )
            return jnp.dot(given[which][slot], window, preferred_element_type=F32)

        def step(index, carry):
            slot = 2 * index
            both = slot + 1 < used
            other = jnp.where(both, slot + 1, slot)
            one, two = product(slot), product(other)
            total[cell_core, meta_ref[cell, 0, slot]] += one
            total[cell_core, meta_ref[cell, 0, other]] += jnp.where(both, two, 0.0)
            return carry

        lax.fori_loop(0, (used + 1) // 2, step, 0)
    n_pair, nodes = out_ref.shape[1], out_ref.shape[4]
    for cell_core in range(2):
        for pair in range(n_pair):
            for high in range(2):
                rows = total[cell_core, high * n_pair + pair].astype(BF16)
                for cell_odd in range(2):
                    out_ref[cell_core, pair, cell_odd, high] = rows[
                        cell_odd * nodes : (cell_odd + 1) * nodes
                    ]


def add(ref):
    total = ref[0].astype(F32)
    for part in range(1, ref.shape[0]):
        total = total + ref[part].astype(F32)
    return total


def repeat_kernel(given_ref, out_ref, sems):
    copies = [
        pltpu.make_async_copy(given_ref, out_ref.at[copy], sems.at[copy])
        for copy in range(out_ref.shape[0])
    ]
    for copy in copies:
        copy.start()
    for copy in copies:
        copy.wait()


def with_bias(main, row):
    high = row.astype(BF16).astype(F32)
    tall = (PAIR, row.shape[1])
    place = lax.broadcasted_iota(jnp.int32, tall, 0)
    high, low = (jnp.broadcast_to(part, tall) for part in (high, row - high))
    side = jnp.where(place == 0, high, jnp.where(place == 1, low, 0.0))
    return jnp.concatenate([main, side], axis=0).astype(BF16)


def bias_of(total):
    depth = total.shape[0] - PAIR
    return total[depth : depth + 1] + total[depth + 1 : depth + 2]


def node_kernel(parts_ref, weight_ref, bias_ref, cot_ref, act_ref, grads_ref):
    n_core, n_pair, n_odd, n_high = parts_ref.shape[:4]
    quarters = []
    for core in range(n_core):
        for odd in range(n_odd):
            senders = [(pair, high) for pair in range(n_pair) for high in range(n_high)]
            total = parts_ref[core, 0, odd, 0].astype(F32)
            for pair, high in senders[1:]:
                total = total + parts_ref[core, pair, odd, high].astype(F32)
            quarters.append(total.astype(BF16))
    aggregated = jnp.concatenate(quarters, axis=1)
    preact = jnp.dot(aggregated, weight_ref[...], preferred_element_type=F32) + bias_ref[...]
    sigmoid_part = jax.nn.sigmoid(preact)
    act_ref[...] = (preact * sigmoid_part).astype(BF16)
    grad = cot_ref[...].astype(F32) * sigmoid_part * (1.0 + preact * (1.0 - sigmoid_part))
    product = lax.dot_general(
        aggregated, grad.astype(BF16), (((0,), (0,)), ((), ())), preferred_element_type=F32
    )
    row = jnp.sum(grad, axis=0, keepdims=True)
    depth = grads_ref.shape[1] - PAIR
    for chunk in range(grads_ref.shape[0]):
        grads_ref[chunk] = with_bias(product[chunk * depth : (chunk + 1) * depth], row)


def scatter_kernel(parts_ref, out_ref):
    total = add(parts_ref)
    depth = out_ref.shape[1] - PAIR
    for chunk in range(out_ref.shape[0]):
        out_ref[chunk] = with_bias(total[chunk * depth : (chunk + 1) * depth], bias_of(total))


def sum_kernel(parts_ref, out_ref):
    total = add(parts_ref)
    rounded = with_bias(total[: total.shape[0] - PAIR], bias_of(total))
    for copy in range(out_ref.shape[0]):
        out_ref[copy] = rounded


def copy_kernel(parts_ref, out_ref):
    depth = parts_ref.shape[1] - PAIR
    parts = [parts_ref[part].astype(F32) for part in range(parts_ref.shape[0])]
    rows = jnp.concatenate([part[:depth] for part in parts] + [parts[0][depth:]], axis=0).astype(BF16)
    for copy in range(out_ref.shape[0]):
        out_ref[copy] = rows


def last_kernel(parts_ref, weight_ref, bias_ref):
    depth = parts_ref.shape[1] - PAIR
    for chunk in range(parts_ref.shape[0]):
        rows = parts_ref[chunk].astype(F32)
        weight_ref[chunk * depth : (chunk + 1) * depth] = rows[:depth]
        if chunk == 0:
            bias_ref[...] = bias_of(rows)


def call(kernel, out, *args, scalars=0):
    shapes = jax.tree.map(lambda o: jax.ShapeDtypeStruct(*o), out, is_leaf=lambda o: isinstance(o[0], tuple) and not isinstance(o[1], tuple))
    specs = jax.tree.map(lambda o: VMEM, shapes)
    return pl.pallas_call(
        kernel, out_shape=shapes, in_specs=[SMEM] * scalars + [VMEM] * (len(args) - scalars), out_specs=specs, compiler_params=PARAMS
    )(*args)


def swap(array, axis):
    return lax.ppermute(array, axis, [(0, 1), (1, 0)])


def per_device(
    features, weight, bias_term, cotangent, tile_values, tile_rows, tile_cols, tile_count
):
    nodes, width = features.shape
    _, _, slots, size, _ = tile_values.shape
    n_z, n_x = lax.axis_size("z_lo"), lax.axis_size("x")
    n_pair = lax.axis_size("y_pair")
    tiles = tile_values[0, 0]
    ints = [tile_rows[0, 0], tile_cols[0, 0], jnp.broadcast_to(tile_count[0], (slots,))]
    side = jnp.pad(jnp.stack(ints), ((0, SIDE - 3), (0, LANES - slots))).astype(BF16)
    quarters = call(quarter_kernel, ((4, nodes + SIDE, LANES), BF16), features, side)
    quarters = lax.all_to_all(quarters, QUAD, 0, 0)
    quarters, tiles = lax.optimization_barrier((quarters, tiles))
    tiles_y = swap(tiles, "y_odd")
    tiles_core = swap(tiles, "core")
    tiles_both = swap(tiles_y, "core")
    meta = quarters[:, nodes : nodes + 3, :slots].astype(jnp.int32)
    near = lax.all_gather(quarters[:, :nodes], "z_lo", axis=0)
    near = pl.pallas_call(
        repeat_kernel,
        out_shape=jax.ShapeDtypeStruct((n_x,) + near.shape, BF16),
        in_specs=[VMEM],
        out_specs=HBM,
        scratch_shapes=[pltpu.SemaphoreType.DMA((n_x,))],
        compiler_params=PARAMS,
    )(near)
    blocks = lax.all_to_all(near, "x", 0, 0)
    place = jnp.stack([lax.axis_index(axis) for axis in QUAD]).astype(jnp.int32)
    term = pl.pallas_call(
        tile_kernel,
        out_shape=jax.ShapeDtypeStruct((2, n_pair, 2, 2, nodes, LANES), BF16),
        in_specs=[SMEM, SMEM] + [VMEM] * 5,
        out_specs=VMEM,
        scratch_shapes=[
            pltpu.VMEM((2, 2 * n_pair, size, LANES), F32),
        ],
        compiler_params=PARAMS,
    )(place, meta, tiles, tiles_y, tiles_core, tiles_both, blocks)
    shares = lax.all_to_all(term.reshape(-1, nodes, LANES), HOME, 0, 0)
    n_near, n_y = lax.axis_size(NEAR), lax.axis_size(Y)
    depth = width // n_near
    tall, short = depth + PAIR, depth // n_y + PAIR
    activations, grads = call(
        node_kernel,
        (((nodes, width), BF16), ((n_near, tall, width), BF16)),
        shares.reshape(2, n_pair, 2, 2, nodes, LANES),
        weight,
        bias_term[None, :],
        cotangent,
    )
    grads = lax.all_to_all(grads, NEAR, 0, 0)
    grads = call(scatter_kernel, ((n_y, short, width), BF16), grads)
    grads = lax.all_to_all(grads, Y, 0, 0)
    grads = call(sum_kernel, ((1, short, width), BF16), grads)
    grads = lax.all_gather(grads[0], Z, axis=0)
    grads = call(sum_kernel, ((1, short, width), BF16), grads)
    grads = lax.all_gather(grads[0], Y, axis=0)
    grads = call(copy_kernel, ((1, tall, width), BF16), grads)
    grads = lax.all_gather(grads[0], NEAR, axis=0)
    weight_grad, bias_grad = call(
        last_kernel, (((width, width), F32), ((1, width), F32)), grads
    )
    return activations, weight_grad, bias_grad[0]


def solution(mesh):
    cut = Mesh(mesh.devices.reshape(SIZES), AXES)
    everywhere = P(AXES, None)
    return jax.shard_map(
        per_device,
        mesh=cut,
        in_specs=(
            everywhere,
            P(),
            P(),
            everywhere,
            P(ROW, COL, None, None, None),
            P(ROW, COL, None),
            P(ROW, COL, None),
            P(ROW, COL),
        ),
        out_specs=(everywhere, P(), P()),
        check_vma=False,
    )
```

```python
import jax
import jax.numpy as jnp
from jax import lax
from jax.experimental import pallas as pl
from jax.experimental.pallas import tpu as pltpu
from jax.sharding import Mesh, PartitionSpec as P

F32 = jnp.float32
BF16 = jnp.bfloat16
LANES = 128
VMEM = pl.BlockSpec(memory_space=pltpu.VMEM)
SMEM = pl.BlockSpec(memory_space=pltpu.SMEM)
HBM = pl.BlockSpec(memory_space=pltpu.HBM)
PARAMS = pltpu.CompilerParams(vmem_limit_bytes=40 * 1024 * 1024)
AXES = ("z_lo", "x", "core", "z_hi", "y_pair", "y_odd")
ROW = ("z_lo", "x", "core")
COL = ("z_hi", "y_pair", "y_odd")
QUAD = ("core", "y_odd")
HOME = ("core", "y_pair", "y_odd", "z_hi")
NEAR = ("x", "core")
Y = ("y_pair", "y_odd")
Z = ("z_lo", "z_hi")
SIZES = (4, 4, 2, 2, 4, 2)
SIDE = 16
PAIR = 8


def lanes_of(part):
    return slice(part * LANES, (part + 1) * LANES)


def quarter_kernel(features_ref, side_ref, out_ref):
    nodes = features_ref.shape[0]
    for part in range(out_ref.shape[0]):
        out_ref[part, :nodes, :] = features_ref[:, lanes_of(part)]
        out_ref[part, nodes:, :] = side_ref[...]


def tile_kernel(place_ref, meta_ref, *refs):
    given, block_ref, out_ref, total = refs[:4], refs[4], refs[5], refs[6]
    n_x = block_ref.shape[0]
    core, odd = place_ref[0], place_ref[1]

    def cell_of(which):
        cell_core, cell_odd = (core + which // 2) % 2, (odd + which % 2) % 2
        return cell_core, cell_odd, cell_core * 2 + cell_odd

    total[...] = jnp.zeros_like(total)
    for which in range(4):
        cell_core, cell_odd, cell = cell_of(which)

        used = meta_ref[cell, 2, 0]

        def product(slot):
            chip = meta_ref[cell, 1, slot]
            z, x = chip // n_x, lax.rem(chip, n_x)
            window = jnp.concatenate(
                [block_ref[x, z, cell_odd], block_ref[x, z, 2 + cell_odd]], axis=0
            )
            return jnp.dot(given[which][slot], window, preferred_element_type=F32)

        def step(index, carry):
            slot = 2 * index
            both = slot + 1 < used
            other = jnp.where(both, slot + 1, slot)
            one, two = product(slot), product(other)
            total[cell_core, meta_ref[cell, 0, slot]] += one
            total[cell_core, meta_ref[cell, 0, other]] += jnp.where(both, two, 0.0)
            return carry

        lax.fori_loop(0, (used + 1) // 2, step, 0)
    n_pair, nodes = out_ref.shape[1], out_ref.shape[4]
    for cell_core in range(2):
        for pair in range(n_pair):
            for high in range(2):
                rows = total[cell_core, high * n_pair + pair].astype(BF16)
                for cell_odd in range(2):
                    out_ref[cell_core, pair, cell_odd, high] = rows[
                        cell_odd * nodes : (cell_odd + 1) * nodes
                    ]


def add(ref):
    total = ref[0].astype(F32)
    for part in range(1, ref.shape[0]):
        total = total + ref[part].astype(F32)
    return total


def repeat_kernel(given_ref, out_ref, sems):
    copies = [
        pltpu.make_async_copy(given_ref, out_ref.at[copy], sems.at[copy])
        for copy in range(out_ref.shape[0])
    ]
    for copy in copies:
        copy.start()
    for copy in copies:
        copy.wait()


def with_bias(main, row):
    high = row.astype(BF16).astype(F32)
    tall = (PAIR, row.shape[1])
    place = lax.broadcasted_iota(jnp.int32, tall, 0)
    high, low = (jnp.broadcast_to(part, tall) for part in (high, row - high))
    side = jnp.where(place == 0, high, jnp.where(place == 1, low, 0.0))
    return jnp.concatenate([main, side], axis=0).astype(BF16)


def bias_of(total):
    depth = total.shape[0] - PAIR
    return total[depth : depth + 1] + total[depth + 1 : depth + 2]


def node_kernel(parts_ref, weight_ref, bias_ref, cot_ref, act_ref, grads_ref):
    n_core, n_pair, n_odd, n_high = parts_ref.shape[:4]
    quarters = []
    for core in range(n_core):
        for odd in range(n_odd):
            senders = [(pair, high) for pair in range(n_pair) for high in range(n_high)]
            total = parts_ref[core, 0, odd, 0].astype(F32)
            for pair, high in senders[1:]:
                total = total + parts_ref[core, pair, odd, high].astype(F32)
            quarters.append(total.astype(BF16))
    aggregated = jnp.concatenate(quarters, axis=1)
    preact = jnp.dot(aggregated, weight_ref[...], preferred_element_type=F32) + bias_ref[...]
    sigmoid_part = jax.nn.sigmoid(preact)
    act_ref[...] = (preact * sigmoid_part).astype(BF16)
    grad = cot_ref[...].astype(F32) * sigmoid_part * (1.0 + preact * (1.0 - sigmoid_part))
    product = lax.dot_general(
        aggregated, grad.astype(BF16), (((0,), (0,)), ((), ())), preferred_element_type=F32
    )
    row = jnp.sum(grad, axis=0, keepdims=True)
    depth = grads_ref.shape[1] - PAIR
    for chunk in range(grads_ref.shape[0]):
        grads_ref[chunk] = with_bias(product[chunk * depth : (chunk + 1) * depth], row)


def beside_bias(main, bias):
    high = bias.astype(BF16).astype(F32)
    side = jnp.concatenate([high, bias - high], axis=0)
    return jnp.concatenate([main, side], axis=1).astype(BF16)


def scatter_kernel(parts_ref, out_ref):
    total = add(parts_ref)
    depth, width = out_ref.shape[1], parts_ref.shape[2]
    row = bias_of(total)
    bias = jnp.concatenate([row[:, lanes_of(part)] for part in range(width // LANES)], axis=0)
    for chunk in range(out_ref.shape[0]):
        out_ref[chunk] = beside_bias(total[chunk * depth : (chunk + 1) * depth], bias)


def sum_kernel(parts_ref, out_ref):
    total = add(parts_ref)
    width = total.shape[1] - LANES
    side = total[:, width:]
    half = side.shape[0] // 2
    rounded = beside_bias(total[:, :width], side[:half] + side[half:])
    for copy in range(out_ref.shape[0]):
        out_ref[copy] = rounded


def copy_kernel(parts_ref, out_ref):
    width = out_ref.shape[2]
    parts = [parts_ref[part].astype(F32) for part in range(parts_ref.shape[0])]
    side = parts[0][:, width:]
    half = side.shape[0] // 2
    bias = side[:half] + side[half:]
    row = jnp.concatenate([bias[part : part + 1] for part in range(half)], axis=1)
    rows = with_bias(jnp.concatenate([part[:, :width] for part in parts], axis=0), row)
    for copy in range(out_ref.shape[0]):
        out_ref[copy] = rows


def last_kernel(parts_ref, weight_ref, bias_ref):
    depth = parts_ref.shape[1] - PAIR
    for chunk in range(parts_ref.shape[0]):
        rows = parts_ref[chunk].astype(F32)
        weight_ref[chunk * depth : (chunk + 1) * depth] = rows[:depth]
        if chunk == 0:
            bias_ref[...] = bias_of(rows)


def call(kernel, out, *args, scalars=0):
    shapes = jax.tree.map(lambda o: jax.ShapeDtypeStruct(*o), out, is_leaf=lambda o: isinstance(o[0], tuple) and not isinstance(o[1], tuple))
    specs = jax.tree.map(lambda o: VMEM, shapes)
    return pl.pallas_call(
        kernel, out_shape=shapes, in_specs=[SMEM] * scalars + [VMEM] * (len(args) - scalars), out_specs=specs, compiler_params=PARAMS
    )(*args)


def swap(array, axis):
    return lax.ppermute(array, axis, [(0, 1), (1, 0)])


def per_device(
    features, weight, bias_term, cotangent, tile_values, tile_rows, tile_cols, tile_count
):
    nodes, width = features.shape
    _, _, slots, size, _ = tile_values.shape
    n_z, n_x = lax.axis_size("z_lo"), lax.axis_size("x")
    n_pair = lax.axis_size("y_pair")
    tiles = tile_values[0, 0]
    ints = [tile_rows[0, 0], tile_cols[0, 0], jnp.broadcast_to(tile_count[0], (slots,))]
    side = jnp.pad(jnp.stack(ints), ((0, SIDE - 3), (0, LANES - slots))).astype(BF16)
    quarters = call(quarter_kernel, ((4, nodes + SIDE, LANES), BF16), features, side)
    quarters = lax.all_to_all(quarters, QUAD, 0, 0)
    quarters, tiles = lax.optimization_barrier((quarters, tiles))
    tiles_y = swap(tiles, "y_odd")
    tiles_core = swap(tiles, "core")
    tiles_both = swap(tiles_y, "core")
    meta = quarters[:, nodes : nodes + 3, :slots].astype(jnp.int32)
    near = lax.all_gather(quarters[:, :nodes], "z_lo", axis=0)
    near = pl.pallas_call(
        repeat_kernel,
        out_shape=jax.ShapeDtypeStruct((n_x,) + near.shape, BF16),
        in_specs=[VMEM],
        out_specs=HBM,
        scratch_shapes=[pltpu.SemaphoreType.DMA((n_x,))],
        compiler_params=PARAMS,
    )(near)
    blocks = lax.all_to_all(near, "x", 0, 0)
    place = jnp.stack([lax.axis_index(axis) for axis in QUAD]).astype(jnp.int32)
    term = pl.pallas_call(
        tile_kernel,
        out_shape=jax.ShapeDtypeStruct((2, n_pair, 2, 2, nodes, LANES), BF16),
        in_specs=[SMEM, SMEM] + [VMEM] * 5,
        out_specs=VMEM,
        scratch_shapes=[
            pltpu.VMEM((2, 2 * n_pair, size, LANES), F32),
        ],
        compiler_params=PARAMS,
    )(place, meta, tiles, tiles_y, tiles_core, tiles_both, blocks)
    shares = lax.all_to_all(term.reshape(-1, nodes, LANES), HOME, 0, 0)
    n_near, n_y, n_deep = lax.axis_size(NEAR), lax.axis_size(Y), lax.axis_size(Z)
    depth = width // n_near
    tall, wide = depth + PAIR, width + LANES
    activations, grads = call(
        node_kernel,
        (((nodes, width), BF16), ((n_near, tall, width), BF16)),
        shares.reshape(2, n_pair, 2, 2, nodes, LANES),
        weight,
        bias_term[None, :],
        cotangent,
    )
    grads = lax.all_to_all(grads, NEAR, 0, 0)
    grads = call(scatter_kernel, ((n_y, depth // n_y, wide), BF16), grads)
    grads = lax.all_to_all(grads, Y, 0, 0)
    grads = call(sum_kernel, ((n_deep, depth // n_y, wide), BF16), grads)
    grads = lax.all_to_all(grads, Z, 0, 0)
    grads = call(sum_kernel, ((n_y, depth // n_y, wide), BF16), grads)
    grads = lax.all_to_all(grads, Y, 0, 0)
    grads = call(copy_kernel, ((n_near, tall, width), BF16), grads)
    grads = lax.all_to_all(grads, NEAR, 0, 0)
    weight_grad, bias_grad = call(
        last_kernel, (((width, width), F32), ((1, width), F32)), grads
    )
    return activations, weight_grad, bias_grad[0]


def solution(mesh):
    cut = Mesh(mesh.devices.reshape(SIZES), AXES)
    everywhere = P(AXES, None)
    return jax.shard_map(
        per_device,
        mesh=cut,
        in_specs=(
            everywhere,
            P(),
            P(),
            everywhere,
            P(ROW, COL, None, None, None),
            P(ROW, COL, None),
            P(ROW, COL, None),
            P(ROW, COL),
        ),
        out_specs=(everywhere, P(), P()),
        check_vma=False,
    )
```

```python
import jax
import jax.numpy as jnp
from jax import lax
from jax.experimental import pallas as pl
from jax.experimental.pallas import tpu as pltpu
from jax.sharding import Mesh, PartitionSpec as P

F32 = jnp.float32
BF16 = jnp.bfloat16
LANES = 128
VMEM = pl.BlockSpec(memory_space=pltpu.VMEM)
SMEM = pl.BlockSpec(memory_space=pltpu.SMEM)
HBM = pl.BlockSpec(memory_space=pltpu.HBM)
PARAMS = pltpu.CompilerParams(vmem_limit_bytes=40 * 1024 * 1024)
AXES = ("z_lo", "x", "core", "z_hi", "y_pair", "y_odd")
ROW = ("z_lo", "x", "core")
COL = ("z_hi", "y_pair", "y_odd")
QUAD = ("core", "y_odd")
HOME = ("core", "y_pair", "y_odd", "z_hi")
NEAR = ("x", "core")
Y = ("y_pair", "y_odd")
Z = ("z_lo", "z_hi")
SIZES = (4, 4, 2, 2, 4, 2)
SIDE = 16
PAIR = 8


def lanes_of(part):
    return slice(part * LANES, (part + 1) * LANES)


def quarter_kernel(features_ref, side_ref, out_ref):
    nodes = features_ref.shape[0]
    for part in range(out_ref.shape[0]):
        out_ref[part, :nodes, :] = features_ref[:, lanes_of(part)]
        out_ref[part, nodes:, :] = side_ref[...]


def tile_kernel(place_ref, meta_ref, *refs):
    given, block_ref, out_ref, total = refs[:4], refs[4], refs[5], refs[6]
    n_x = block_ref.shape[0]
    core, odd = place_ref[0], place_ref[1]

    def cell_of(which):
        cell_core, cell_odd = (core + which // 2) % 2, (odd + which % 2) % 2
        return cell_core, cell_odd, cell_core * 2 + cell_odd

    total[...] = jnp.zeros_like(total)
    for which in range(4):
        cell_core, cell_odd, cell = cell_of(which)

        used = meta_ref[cell, 2, 0]

        def product(slot):
            chip = meta_ref[cell, 1, slot]
            z, x = chip // n_x, lax.rem(chip, n_x)
            window = jnp.concatenate(
                [block_ref[x, z, cell_odd], block_ref[x, z, 2 + cell_odd]], axis=0
            )
            return jnp.dot(given[which][slot], window, preferred_element_type=F32)

        def step(index, carry):
            slot = 2 * index
            both = slot + 1 < used
            other = jnp.where(both, slot + 1, slot)
            one, two = product(slot), product(other)
            total[cell_core, meta_ref[cell, 0, slot]] += one
            total[cell_core, meta_ref[cell, 0, other]] += jnp.where(both, two, 0.0)
            return carry

        lax.fori_loop(0, (used + 1) // 2, step, 0)
    n_pair, nodes = out_ref.shape[1], out_ref.shape[4]
    for cell_core in range(2):
        for pair in range(n_pair):
            for high in range(2):
                rows = total[cell_core, high * n_pair + pair].astype(BF16)
                for cell_odd in range(2):
                    out_ref[cell_core, pair, cell_odd, high] = rows[
                        cell_odd * nodes : (cell_odd + 1) * nodes
                    ]


def add(ref):
    total = ref[0].astype(F32)
    for part in range(1, ref.shape[0]):
        total = total + ref[part].astype(F32)
    return total


def repeat_kernel(given_ref, out_ref, sems):
    copies = [
        pltpu.make_async_copy(given_ref, out_ref.at[copy], sems.at[copy])
        for copy in range(out_ref.shape[0])
    ]
    for copy in copies:
        copy.start()
    for copy in copies:
        copy.wait()


def with_bias(main, row):
    high = row.astype(BF16).astype(F32)
    tall = (PAIR, row.shape[1])
    place = lax.broadcasted_iota(jnp.int32, tall, 0)
    high, low = (jnp.broadcast_to(part, tall) for part in (high, row - high))
    side = jnp.where(place == 0, high, jnp.where(place == 1, low, 0.0))
    return jnp.concatenate([main, side], axis=0).astype(BF16)


def bias_of(total):
    depth = total.shape[0] - PAIR
    return total[depth : depth + 1] + total[depth + 1 : depth + 2]


def node_kernel(parts_ref, weight_ref, bias_ref, cot_ref, act_ref, grads_ref):
    n_core, n_pair, n_odd, n_high = parts_ref.shape[:4]
    quarters = []
    for core in range(n_core):
        for odd in range(n_odd):
            senders = [(pair, high) for pair in range(n_pair) for high in range(n_high)]
            total = parts_ref[core, 0, odd, 0].astype(F32)
            for pair, high in senders[1:]:
                total = total + parts_ref[core, pair, odd, high].astype(F32)
            quarters.append(total.astype(BF16))
    aggregated = jnp.concatenate(quarters, axis=1)
    preact = jnp.dot(aggregated, weight_ref[...], preferred_element_type=F32) + bias_ref[...]
    sigmoid_part = jax.nn.sigmoid(preact)
    act_ref[...] = (preact * sigmoid_part).astype(BF16)
    grad = cot_ref[...].astype(F32) * sigmoid_part * (1.0 + preact * (1.0 - sigmoid_part))
    product = lax.dot_general(
        aggregated, grad.astype(BF16), (((0,), (0,)), ((), ())), preferred_element_type=F32
    )
    row = jnp.sum(grad, axis=0, keepdims=True)
    depth = grads_ref.shape[1] - PAIR
    for chunk in range(grads_ref.shape[0]):
        grads_ref[chunk] = with_bias(product[chunk * depth : (chunk + 1) * depth], row)


def beside_bias(main, bias):
    high = bias.astype(BF16).astype(F32)
    side = jnp.concatenate([high, bias - high], axis=0)
    return jnp.concatenate([main, side], axis=1).astype(BF16)


def scatter_kernel(parts_ref, out_ref):
    total = add(parts_ref)
    depth, width = out_ref.shape[1], parts_ref.shape[2]
    row = bias_of(total)
    bias = jnp.concatenate([row[:, lanes_of(part)] for part in range(width // LANES)], axis=0)
    for chunk in range(out_ref.shape[0]):
        out_ref[chunk] = beside_bias(total[chunk * depth : (chunk + 1) * depth], bias)


def sum_kernel(parts_ref, out_ref):
    total = add(parts_ref)
    width = total.shape[1] - LANES
    side = total[:, width:]
    half = side.shape[0] // 2
    rounded = beside_bias(total[:, :width], side[:half] + side[half:])
    for copy in range(out_ref.shape[0]):
        out_ref[copy] = rounded


def copy_kernel(parts_ref, out_ref):
    width = out_ref.shape[2]
    parts = [parts_ref[part].astype(F32) for part in range(parts_ref.shape[0])]
    side = parts[0][:, width:]
    half = side.shape[0] // 2
    bias = side[:half] + side[half:]
    row = jnp.concatenate([bias[part : part + 1] for part in range(half)], axis=1)
    rows = with_bias(jnp.concatenate([part[:, :width] for part in parts], axis=0), row)
    for copy in range(out_ref.shape[0]):
        out_ref[copy] = rows


def last_kernel(parts_ref, weight_ref, bias_ref):
    depth = parts_ref.shape[1] - PAIR
    for chunk in range(parts_ref.shape[0]):
        rows = parts_ref[chunk].astype(F32)
        weight_ref[chunk * depth : (chunk + 1) * depth] = rows[:depth]
        if chunk == 0:
            bias_ref[...] = bias_of(rows)


def call(kernel, out, *args, scalars=0):
    shapes = jax.tree.map(lambda o: jax.ShapeDtypeStruct(*o), out, is_leaf=lambda o: isinstance(o[0], tuple) and not isinstance(o[1], tuple))
    specs = jax.tree.map(lambda o: VMEM, shapes)
    return pl.pallas_call(
        kernel, out_shape=shapes, in_specs=[SMEM] * scalars + [VMEM] * (len(args) - scalars), out_specs=specs, compiler_params=PARAMS
    )(*args)


def swap(array, axis):
    return lax.ppermute(array, axis, [(0, 1), (1, 0)])


def per_device(
    features, weight, bias_term, cotangent, tile_values, tile_rows, tile_cols, tile_count
):
    nodes, width = features.shape
    _, _, slots, size, _ = tile_values.shape
    n_z, n_x = lax.axis_size("z_lo"), lax.axis_size("x")
    n_pair = lax.axis_size("y_pair")
    tiles = tile_values[0, 0]
    ints = [tile_rows[0, 0], tile_cols[0, 0], jnp.broadcast_to(tile_count[0], (slots,))]
    side = jnp.pad(jnp.stack(ints), ((0, SIDE - 3), (0, LANES - slots))).astype(BF16)
    quarters = call(quarter_kernel, ((4, nodes + SIDE, LANES), BF16), features, side)
    quarters = lax.all_to_all(quarters, QUAD, 0, 0)
    quarters, tiles = lax.optimization_barrier((quarters, tiles))
    tiles_y = swap(tiles, "y_odd")
    tiles_core = swap(tiles, "core")
    tiles_both = swap(tiles_y, "core")
    meta = quarters[:, nodes : nodes + 3, :slots].astype(jnp.int32)
    near = lax.all_gather(quarters[:, :nodes], "z_lo", axis=0)
    near = pl.pallas_call(
        repeat_kernel,
        out_shape=jax.ShapeDtypeStruct((n_x,) + near.shape, BF16),
        in_specs=[VMEM],
        out_specs=HBM,
        scratch_shapes=[pltpu.SemaphoreType.DMA((n_x,))],
        compiler_params=PARAMS,
    )(near)
    blocks = lax.all_to_all(near, "x", 0, 0)
    place = jnp.stack([lax.axis_index(axis) for axis in QUAD]).astype(jnp.int32)
    term = pl.pallas_call(
        tile_kernel,
        out_shape=jax.ShapeDtypeStruct((2, n_pair, 2, 2, nodes, LANES), BF16),
        in_specs=[SMEM, SMEM] + [VMEM] * 5,
        out_specs=VMEM,
        scratch_shapes=[
            pltpu.VMEM((2, 2 * n_pair, size, LANES), F32),
        ],
        compiler_params=PARAMS,
    )(place, meta, tiles, tiles_y, tiles_core, tiles_both, blocks)
    shares = lax.all_to_all(term.reshape(-1, nodes, LANES), HOME, 0, 0)
    n_near, n_deep, n_y = lax.axis_size(NEAR), lax.axis_size(Z), lax.axis_size(Y)
    depth = width // n_near
    tall, wide = depth + PAIR, width + LANES
    activations, grads = call(
        node_kernel,
        (((nodes, width), BF16), ((n_near, tall, width), BF16)),
        shares.reshape(2, n_pair, 2, 2, nodes, LANES),
        weight,
        bias_term[None, :],
        cotangent,
    )
    grads = lax.all_to_all(grads, NEAR, 0, 0)
    grads = call(scatter_kernel, ((n_deep, depth // n_deep, wide), BF16), grads)
    grads = lax.all_to_all(grads, Z, 0, 0)
    grads = call(sum_kernel, ((n_y, depth // n_deep, wide), BF16), grads)
    grads = lax.all_to_all(grads, Y, 0, 0)
    grads = call(sum_kernel, ((n_deep, depth // n_deep, wide), BF16), grads)
    grads = lax.all_to_all(grads, Z, 0, 0)
    grads = call(copy_kernel, ((n_near, tall, width), BF16), grads)
    grads = lax.all_to_all(grads, NEAR, 0, 0)
    weight_grad, bias_grad = call(
        last_kernel, (((width, width), F32), ((1, width), F32)), grads
    )
    return activations, weight_grad, bias_grad[0]


def solution(mesh):
    cut = Mesh(mesh.devices.reshape(SIZES), AXES)
    everywhere = P(AXES, None)
    return jax.shard_map(
        per_device,
        mesh=cut,
        in_specs=(
            everywhere,
            P(),
            P(),
            everywhere,
            P(ROW, COL, None, None, None),
            P(ROW, COL, None),
            P(ROW, COL, None),
            P(ROW, COL),
        ),
        out_specs=(everywhere, P(), P()),
        check_vma=False,
    )
```
